32 devices in a mesh: groups: 2 (over x), chan: 16 (over z, y, core).
Axes of the slice: x: 2, y: 2, z: 4, core: 2. Of those that a mesh axis runs over, the one named last changes fastest.
Arguments:
- raw: bfloat16 [5120, 4096], P('chan', 'groups'), parts along dimension 1, may hold values from -50 to 50
- taps: bfloat16 [255], replicated, may hold values from -0.375 to 0.375
- tile_dist: int32 [16, 8], P('chan', 'groups'), parts along dimension 1, may hold values from 1 to 4, as said below
- tile_count: int32 [32], P(('groups', 'chan')), parts along dimension 0, may hold values from 0 to 4
- owner: int32 [8], P('groups'), parts along dimension 0, may hold values from 0 to 15, as said below
Outputs:
- band_stack: float32 [16, 256, 128], P('chan', 'groups'), parts along dimension 1
The draws below stay inside these ranges and needn't reach their ends.
There are 2 independent parts, one for each index of `groups`. The reference program is written for one: setup_inputs(seed, part) draws one part's arguments, and reference() takes and returns one part's arrays. A program takes and returns all parts, laid end to end along the dimension named above; an argument that names none is the same for every part. Nothing has to cross between parts.
Inputs may be any that keep to these rules, and one draw needn't show every extreme that they name: Each row of tile_dist holds every distance of 1 to 4 once; in row i the first tile_count[i] entries d satisfy i + d < 16. `owner`: the owners are distinct, and some band is owned by index 15.
All inputs are finite; a program needn't handle non-finite values.
Results may differ from the reference program's by a relative error of at most 0.014.
Values may be sent and summed in bfloat16 or wider, within the bound.
A program may use at most 128 MiB of HBM per device.

```python
import math
import jax
import jax.numpy as jnp
from jax import lax

CB = 128
NB = 4
TAPS = 255
CH = 2048
TIME = 5120
BINS = 64
HALF = 127
N_CHAN = 16


def draw_raw(key, part):
    first, second = jax.random.split(key, 2)
    level = jnp.exp(jax.random.uniform(first, (1, CH), jnp.float32, 0.0, math.log(10.0)))
    noise = jnp.clip(jax.random.normal(second, (TIME, CH), jnp.float32), -5.0, 5.0)
    return (noise * level).astype(jnp.bfloat16)


def tile_plan(key):
    base = jax.random.fold_in(key, 7)
    ranks = jax.random.randint(jax.random.fold_in(base, 1), (N_CHAN, NB), 0, 1 << 20)
    lanes = jnp.arange(NB, dtype=jnp.int32)
    device = jnp.arange(N_CHAN, dtype=jnp.int32)[:, None]
    invalid = (device + lanes[None, :] + 1 >= N_CHAN).astype(jnp.int32)
    score = invalid * (1 << 28) + ranks * NB + lanes[None, :]
    order = jnp.argsort(score, axis=1).astype(jnp.int32)
    distances = order + 1
    usable = NB - jnp.sum(invalid, axis=1)
    draws = jax.random.randint(jax.random.fold_in(base, 2), (N_CHAN,), 0, NB)
    counts = 1 + draws * draws * (NB - 1) // ((NB - 1) * (NB - 1))
    counts = jnp.where(device[:, 0] == 0, NB, counts)
    counts = jnp.minimum(counts, usable).astype(jnp.int32)
    return (distances, counts)


def draw_tile_dist(key, part):
    return tile_plan(key)[0]


def draw_tile_count(key, part):
    return tile_plan(key)[1]


def draw_owner(key, part):
    others = jax.random.permutation(jax.random.fold_in(key, 19), N_CHAN - 1)[:NB - 1].astype(jnp.int32)
    values = jnp.concatenate([others, jnp.full((1,), N_CHAN - 1, jnp.int32)])
    order = jax.random.permutation(jax.random.fold_in(key, 23), NB).astype(jnp.int32)
    return values[order].astype(jnp.int32)


def bell_draw(own_key, dims, spread, bound, kind=jnp.bfloat16):
    values = jax.random.normal(own_key, dims, jnp.float32) * spread
    return jnp.minimum(jnp.maximum(values, -bound), bound).astype(kind)


def setup_inputs(seed: int = 0, part: int = 0) -> dict:
    streams_of = jax.random.split(jax.random.key(seed), 6)
    own_keys = jax.random.split(jax.random.fold_in(streams_of[5], part), 6)
    raw = draw_raw(jax.random.fold_in(jax.random.fold_in(streams_of[5], part), 71), part)
    taps = bell_draw(streams_of[1], (TAPS,), TAPS ** -0.5, 0.375)
    tile_dist = draw_tile_dist(jax.random.fold_in(jax.random.fold_in(streams_of[5], part), 71), part)
    tile_count = draw_tile_count(jax.random.fold_in(jax.random.fold_in(streams_of[5], part), 71), part)
    owner = draw_owner(jax.random.fold_in(jax.random.fold_in(streams_of[5], part), 71), part)
    return dict(raw=raw, taps=taps, tile_dist=tile_dist, tile_count=tile_count, owner=owner)


def reference(raw, taps, tile_dist, tile_count, owner):
    length = 1 << (TIME + TAPS - 2).bit_length()
    flipped = taps.astype(jnp.float32)[::-1]
    response = jnp.fft.rfft(flipped, length)

    def block_spectra(index):
        start = (index * CB).astype(jnp.int32)
        block = lax.dynamic_slice_in_dim(raw, start, CB, 1).astype(jnp.float32)
        full = jnp.fft.irfft(jnp.fft.rfft(block, length, axis=0) * response[:, None], length, axis=0)
        decimated = full[HALF:HALF + TIME:5].astype(jnp.float32).astype(jnp.bfloat16)
        spectrum = jnp.fft.rfft(decimated.astype(jnp.float32), axis=0)[1:BINS + 1]
        real_part = jnp.real(spectrum).astype(jnp.float32)
        imag_part = jnp.imag(spectrum).astype(jnp.float32)
        stacked = jnp.concatenate([real_part, imag_part], axis=0)
        power = lax.optimization_barrier(jnp.sum(real_part * real_part + imag_part * imag_part, axis=1)) / (2 * CB)
        gain = lax.rsqrt(power + 1e-06)
        return (stacked * jnp.concatenate([gain, gain])[:, None]).astype(jnp.bfloat16)
    spectra = lax.map(block_spectra, jnp.arange(N_CHAN, dtype=jnp.int32))
    slots = jnp.arange(NB, dtype=jnp.int32)[None, :] < tile_count[:, None]
    scale = 1.0 / (2 * BINS)
    stacks = []
    for distance in range(1, NB + 1):
        listed = lax.optimization_barrier(jnp.sum((slots & (tile_dist == distance)).astype(jnp.float32), axis=1))
        left = spectra[:N_CHAN - distance].astype(jnp.float32) * listed[:N_CHAN - distance, None, None]
        right = spectra[distance:].astype(jnp.float32)
        stacks.append(jnp.einsum('iea,ieb->ab', left, right, precision=lax.Precision.HIGHEST) * scale)
    stacked = jnp.stack(stacks)
    places = (owner[:, None] == jnp.arange(N_CHAN, dtype=jnp.int32)[None, :]).astype(jnp.float32)
    return jnp.einsum('bn,bxy->nxy', places, stacked, precision=lax.Precision.HIGHEST)
```

```python
import functools
import math

import jax
import jax.numpy as jnp
from jax import lax
from jax.experimental import pallas as pl
from jax.experimental.pallas import tpu as pltpu
from jax.sharding import PartitionSpec as P

MESH = pl.DeviceIdType.MESH


def extended(x, sides, width):
    for axis, dim in sides:
        size, length = (lax.axis_size(axis), x.shape[dim])
        up = [(i, (i + 1) % size) for i in range(size - 1)]
        down = [(j, i) for i, j in up]
        last = lax.slice_in_dim(x, length - width, length, axis=dim)
        initial = lax.slice_in_dim(x, 0, width, axis=dim)
        before = lax.ppermute(last, axis, up)
        after = lax.ppermute(initial, axis, down)
        x = jnp.concatenate([before, x, after], axis=dim)
    return x


def passed_along(x, axis, by):
    size = lax.axis_size(axis)
    pairs = [(i, i + by) for i in range(size) if 0 <= i + by < size]
    return lax.ppermute(x, axis, pairs)


def band_matrix(taps, out_rows, in_cols):
    period = in_cols + 5
    padded = jnp.pad(taps, (0, period - taps.shape[0]))
    return jnp.tile(padded, out_rows)[: out_rows * in_cols].reshape(out_rows, in_cols)


def whiten(block):
    length, channels = block.shape
    bins = length // 16
    freqs = jnp.arange(1, bins + 1, dtype=jnp.int32)[:, None]
    times = jnp.arange(length, dtype=jnp.int32)[None, :]
    angle = (freqs * times % length).astype(jnp.float32) * (2.0 * math.pi / length)
    table = jnp.concatenate([jnp.cos(angle), -jnp.sin(angle)], axis=0)
    table_high = table.astype(jnp.bfloat16)
    table_low = (table - table_high.astype(jnp.float32)).astype(jnp.bfloat16)
    spectrum = jnp.dot(table_high, block, preferred_element_type=jnp.float32)
    spectrum = spectrum + jnp.dot(table_low, block, preferred_element_type=jnp.float32)
    squares = spectrum * spectrum
    power = jnp.sum(squares[:bins] + squares[bins:], axis=1) / (2 * channels)
    gain = lax.rsqrt(power + 1e-06)
    return (spectrum * jnp.concatenate([gain, gain])[:, None]).astype(jnp.bfloat16)


def cross_tile(mine, partner, scale):
    product = lax.dot_general(
        mine, partner, (((0,), (0,)), ((), ())), preferred_element_type=jnp.float32
    )
    return product * scale


def streamed(raw, taps, tile_dist, tile_count, owner):
    rows = raw.shape[0]
    width = taps.shape[0]
    half = (width - 1) // 2
    out_rows = rows // 5
    banded = band_matrix(taps, out_rows, rows + 2 * half)
    padded = extended(raw, (("chan", 0),), half)
    filtered = jnp.dot(banded, padded, preferred_element_type=jnp.float32)
    decimated = filtered.astype(jnp.bfloat16)
    regrouped = lax.all_to_all(decimated, "chan", split_axis=1, concat_axis=0, tiled=True)
    whitened = whiten(regrouped)
    channels = whitened.shape[1]
    scale = 1.0 / whitened.shape[0]
    bands = tile_dist.shape[1]
    slots = jnp.arange(bands, dtype=jnp.int32) < tile_count[0]
    stacks = []
    for distance in range(1, bands + 1):
        partner = passed_along(whitened, "chan", -distance)
        listed = jnp.sum(((tile_dist[0] == distance) & slots).astype(jnp.int32))
        tile = lax.cond(
            listed > 0,
            lambda first, second: cross_tile(first, second, scale),
            lambda first, second: jnp.zeros((channels, channels), jnp.float32),
            whitened,
            partner,
        )
        stacks.append(tile)
    stacked = jnp.stack(stacks)
    totals = lax.psum(stacked, "chan")
    selected = (owner == lax.axis_index("chan")).astype(jnp.float32)
    return jnp.einsum("b,bxy->xy", selected, totals, precision=lax.Precision.HIGHEST)[None]


def split(x):
    high = x.astype(jnp.bfloat16)
    low = (x - high.astype(jnp.float32)).astype(jnp.bfloat16)
    return high, low


def mm(a, b):
    return jnp.dot(a, b, preferred_element_type=jnp.float32)


def fused_kernel(
    n, bands, pieces,
    raw_hbm, taps_hbm, dist_hbm, count_hbm, owner_hbm, out_ref,
    raw_ref, taps_ref, dist_ref, count_ref, owner_ref, loads, smalls,
    both, pair, send1, recv1, gath, ss0, rs0, ss1, rs1, ss2, rs2, ss3, rs3, ss4, rs4,
):
    me = lax.axis_index("chan")
    chips = n // 2
    chip, core = me // 2, me % 2
    other = chip * 2 + 1 - core
    rows, channels = raw_ref.shape
    block = channels // n
    steps = rows // 5
    length = steps * n
    bins = length // 16
    mine = 2 * bins // n
    hc = channels // 2
    width = hc // pieces
    window = 128
    lead = (window - steps) // 2
    half = (taps_hbm.shape[0] - 1) // 2
    lanes = 1024
    start = lanes - 5 * lead - half

    small = [
        pltpu.make_async_copy(source, held, smalls.at[at])
        for at, (source, held) in enumerate(
            [
                (taps_hbm, taps_ref),
                (dist_hbm, dist_ref),
                (count_hbm, count_ref),
                (owner_hbm, owner_ref),
            ]
        )
    ]
    for load in small:
        load.start()

    def load(p, h):
        cols = pl.ds(h * hc + p * width, width)
        return pltpu.make_async_copy(
            raw_hbm.at[:, cols], raw_ref.at[:, cols], loads.at[2 * p + h]
        )

    for p in range(pieces):
        for h in range(2):
            load(p, h).start()

    z, y = chip // 2, chip % 2

    def peer(k):
        far = [z, z + 1 - 2 * (z % 2), lax.rem(z + 2, 4), 3 - z][k // 2]
        return far * 2 + (1 - y if k % 2 else y)

    order = list(range(chips - 1, 0, -1))
    barrier = pltpu.get_barrier_semaphore()
    for k in order:
        pl.semaphore_signal(
            barrier, inc=1, device_id={"chan": peer(k) * 2 + core}, device_id_type=MESH
        )
    pl.semaphore_signal(barrier, inc=1, device_id={"chan": other}, device_id_type=MESH)

    row = lax.broadcasted_iota(jnp.int32, (2 * bins, window), 0)
    col = lax.broadcasted_iota(jnp.int32, (2 * bins, window), 1)
    place = row % mine
    rank = row // mine
    holder = (rank % chips) * 2 + rank // chips
    freq = holder * (mine // 2) + place % (mine // 2) + 1
    time = me * steps - lead + col
    turn = (freq * time + jnp.where(place >= mine // 2, length // 4, 0)) & (length - 1)
    table = jnp.cos(turn.astype(jnp.float32) * (2.0 * math.pi / length))
    table = jnp.where((time >= 0) & (time < length), table, 0.0)
    table_high, table_low = split(table)

    for load_one in small:
        load_one.wait()
    tap = taps_ref[...].astype(jnp.float32).reshape(1, -1)
    line = jnp.concatenate(
        [
            jnp.zeros((1, start), jnp.float32),
            tap,
            jnp.zeros((1, lanes - start - tap.shape[1]), jnp.float32),
        ],
        axis=1,
    )
    first = pltpu.roll(jnp.broadcast_to(line, (8, lanes)), 0, 1, stride=5, stride_axis=0)
    banded = jnp.concatenate(
        [pltpu.roll(first, 40 * q, 1)[:, :384] for q in range(window // 8)], axis=0
    ).astype(jnp.bfloat16)[:, :rows]
    gmap = mm(table_high, banded) + mm(table_low, banded)
    gmap_high, gmap_low = split(gmap)

    lines = lax.broadcasted_iota(jnp.int32, (2 * mine, 128), 0)
    info = jnp.zeros((2 * mine, 128), jnp.float32)
    for d in range(bands):
        listed = jnp.int32(0)
        for s in range(bands):
            hit = (dist_ref[0, s] == d + 1) & (s < count_ref[0])
            listed = listed + hit.astype(jnp.int32)
        info = jnp.where(lines == core * mine + d, listed.astype(jnp.float32), info)
    both[:, :, hc:] = jnp.broadcast_to(info[None], (n, 2 * mine, 128)).astype(jnp.bfloat16)
    chosen = [(owner_ref[d] == me).astype(jnp.float32) for d in range(bands)]

    def transform(p):
        halves = []
        for h in range(2):
            load(p, h).wait()
            part = raw_ref[:, h * hc + p * width : h * hc + (p + 1) * width]
            spectra = mm(gmap_high, part) + mm(gmap_low, part)
            halves.append(spectra.reshape(n, mine, width))
        both[:, :, p * width : (p + 1) * width] = jnp.concatenate(halves, axis=1).astype(
            jnp.bfloat16
        )

    def span(p, extra=128):
        return p * width, width + (extra if p == pieces - 1 else 0)

    def copy0(p):
        cols = pl.ds(*span(p))
        return pltpu.make_async_remote_copy(
            src_ref=both.at[pl.ds((1 - core) * chips, chips), :, cols],
            dst_ref=pair.at[:, :, cols], send_sem=ss0.at[p], recv_sem=rs0.at[p],
            device_id={"chan": other}, device_id_type=MESH,
        )

    def copy1(p, k):
        cols = pl.ds(*span(p))
        return pltpu.make_async_remote_copy(
            src_ref=send1.at[peer(k), :, cols], dst_ref=recv1.at[chip, :, cols],
            send_sem=ss1.at[p * chips + k], recv_sem=rs1.at[p * chips + k],
            device_id={"chan": peer(k) * 2 + core}, device_id_type=MESH,
        )

    def copy2(p, k):
        cols = pl.ds(*span(p, 0))
        return pltpu.make_async_remote_copy(
            src_ref=gath.at[me, :, cols], dst_ref=gath.at[me, :, cols],
            send_sem=ss2.at[p * chips + k], recv_sem=rs2.at[p * chips + k],
            device_id={"chan": peer(k) * 2 + core}, device_id_type=MESH,
        )

    def copy3(p, k):
        cols = pl.ds(*span(p, 0))
        source = peer(k) * 2 + core
        return pltpu.make_async_remote_copy(
            src_ref=gath.at[source, :, cols], dst_ref=gath.at[source, :, cols],
            send_sem=ss3.at[p * chips + k], recv_sem=rs3.at[p * chips + k],
            device_id={"chan": other}, device_id_type=MESH,
        )

    def copy4(p):
        cols = pl.ds(*span(p, 0))
        return pltpu.make_async_remote_copy(
            src_ref=gath.at[me, :, cols], dst_ref=gath.at[me, :, cols],
            send_sem=ss4.at[p], recv_sem=rs4.at[p],
            device_id={"chan": other}, device_id_type=MESH,
        )

    for p in range(pieces):
        transform(p)
    pl.semaphore_wait(barrier, chips)
    for p in range(pieces):
        copy0(p).start()
    for p in range(pieces):
        at, size = span(p)
        cols = slice(at, at + size)
        copy0(p).wait_recv()
        for k in order:
            to = peer(k)
            own = both[core * chips + to, :, cols].astype(jnp.float32)
            send1[to, :, cols] = (own + pair[to, :, cols].astype(jnp.float32)).astype(jnp.bfloat16)
            copy1(p, k).start()
        own = both[core * chips + chip, :, cols].astype(jnp.float32)
        recv1[chip, :, cols] = (own + pair[chip, :, cols].astype(jnp.float32)).astype(jnp.bfloat16)

    for p in range(pieces):
        for k in order:
            copy1(p, k).wait_recv()
        cols = slice(p * width, (p + 1) * width)
        total = recv1[0, :, cols].astype(jnp.float32)
        for i in range(1, chips):
            total = total + recv1[i, :, cols].astype(jnp.float32)
        squares = total * total
        white = []
        for b in range(width // block):
            at = slice(b * block, (b + 1) * block)
            power = jnp.sum(squares[:, at], axis=1, keepdims=True)
            turned = [
                pltpu.roll(power[h * mine : (h + 1) * mine], mine // 2, 0) for h in range(2)
            ]
            power = (power + jnp.concatenate(turned, axis=0)) / (2 * block)
            white.append(total[:, at] * lax.rsqrt(power + 1e-06))
        gath[me, :, cols] = jnp.concatenate(white, axis=1).astype(jnp.bfloat16)
        for k in order:
            copy2(p, k).start()
        copy4(p).start()

    weights = []
    for i in range(n):
        weight = jnp.zeros((1, 128), jnp.float32)
        for d in range(bands):
            at = i % 2 * mine + d
            weight = weight + recv1[i // 2, at : at + 1, hc:].astype(jnp.float32) * chosen[d]
        weights.append(jnp.broadcast_to(weight, (mine, block)))
    scales = [
        jnp.concatenate([weights[t], weights[t + n // 2]], axis=0) for t in range(n // 2)
    ]

    def products(source):
        held = gath[source].astype(jnp.float32)
        tiles = [held[:, t * block : (t + 1) * block] for t in range(n // 2)]
        left = [tiles[t] * scales[t] for t in range(n // 2)]
        for d in range(bands):
            tiles.append(
                jnp.concatenate([tiles[d][mine:], jnp.zeros((mine, block), jnp.float32)], axis=0)
            )
        right = []
        for t in range(n // 2):
            tile = tiles[t + 1] * chosen[0]
            for d in range(1, bands):
                tile = tile + tiles[t + d + 1] * chosen[d]
            right.append(tile)
        return left, right

    def add(total, at):
        left0, right0 = products(at * 2)
        left1, right1 = products(at * 2 + 1)
        left = jnp.concatenate(left0 + left1, axis=0).astype(jnp.bfloat16)
        right = jnp.concatenate(right0 + right1, axis=0).astype(jnp.bfloat16)
        return total + lax.dot_general(
            left, right, (((0,), (0,)), ((), ())), preferred_element_type=jnp.float32
        )

    near = order[::-1]
    for p in range(pieces):
        copy4(p).wait_recv()
        for k in near:
            copy2(p, k).wait_recv()
            copy3(p, k).start()
    result = add(jnp.zeros((block, block), jnp.float32), chip)
    for k in near:
        for p in range(pieces):
            copy3(p, k).wait_recv()
        result = add(result, peer(k))
    out_ref[0] = result * (1.0 / (2 * bins))

    for p in range(pieces):
        copy0(p).wait_send()
        copy4(p).wait_send()
        for k in order:
            copy1(p, k).wait_send()
            copy2(p, k).wait_send()
            copy3(p, k).wait_send()


def fused(raw, taps, tile_dist, tile_count, owner):
    n = lax.axis_size("chan")
    rows, channels = raw.shape
    bands = tile_dist.shape[1]
    block = channels // n
    steps = rows // 5
    mine = 2 * (steps * n // 16) // n
    chips = n // 2
    hc = channels // 2
    pieces = 4
    vmem, hbm = pl.BlockSpec(memory_space=pltpu.VMEM), pl.BlockSpec(memory_space=pltpu.HBM)
    dma = pltpu.SemaphoreType.DMA
    return pl.pallas_call(
        functools.partial(fused_kernel, n, bands, pieces),
        out_shape=jax.ShapeDtypeStruct((1, block, block), jnp.float32),
        in_specs=[hbm] * 5,
        out_specs=vmem,
        scratch_shapes=[
            pltpu.VMEM(raw.shape, raw.dtype),
            pltpu.VMEM(taps.shape, taps.dtype),
            pltpu.SMEM(tile_dist.shape, jnp.int32),
            pltpu.SMEM(tile_count.shape, jnp.int32),
            pltpu.SMEM(owner.shape, jnp.int32),
            dma((2 * pieces,)),
            dma((4,)),
            pltpu.VMEM((n, 2 * mine, hc + 128), jnp.bfloat16),
            pltpu.VMEM((chips, 2 * mine, hc + 128), jnp.bfloat16),
            pltpu.VMEM((chips, 2 * mine, hc + 128), jnp.bfloat16),
            pltpu.VMEM((chips, 2 * mine, hc + 128), jnp.bfloat16),
            pltpu.VMEM((n, 2 * mine, hc), jnp.bfloat16),
            dma((pieces,)),
            dma((pieces,)),
            dma((pieces * chips,)),
            dma((pieces * chips,)),
            dma((pieces * chips,)),
            dma((pieces * chips,)),
            dma((pieces * chips,)),
            dma((pieces * chips,)),
            dma((pieces,)),
            dma((pieces,)),
        ],
        compiler_params=pltpu.CompilerParams(
            collective_id=0, has_side_effects=True, vmem_limit_bytes=int(53.25 * 2**20)
        ),
    )(raw, taps, tile_dist, tile_count, owner)


def shards(raw, taps, tile_dist, tile_count, owner):
    n = lax.axis_size("chan")
    rows, channels = raw.shape
    steps = rows // 5
    fits = (
        channels == 128 * n
        and n == 16
        and rows == 320
        and taps.shape[0] == 255
        and tile_dist.shape[1] == 4
    )
    path = fused if fits else streamed
    return path(raw, taps, tile_dist, tile_count, owner)


def solution(mesh):
    in_specs = (P("chan", "groups"), P(), P("chan", "groups"), P(("groups", "chan")), P("groups"))
    out_specs = P("chan", "groups", None)
    return jax.shard_map(shards, mesh=mesh, in_specs=in_specs, out_specs=out_specs, check_vma=False)
```

```python
import functools
import math

import jax
import jax.numpy as jnp
from jax import lax
from jax.experimental import pallas as pl
from jax.experimental.pallas import tpu as pltpu
from jax.sharding import PartitionSpec as P

MESH = pl.DeviceIdType.MESH


def extended(x, sides, width):
    for axis, dim in sides:
        size, length = (lax.axis_size(axis), x.shape[dim])
        up = [(i, (i + 1) % size) for i in range(size - 1)]
        down = [(j, i) for i, j in up]
        last = lax.slice_in_dim(x, length - width, length, axis=dim)
        initial = lax.slice_in_dim(x, 0, width, axis=dim)
        before = lax.ppermute(last, axis, up)
        after = lax.ppermute(initial, axis, down)
        x = jnp.concatenate([before, x, after], axis=dim)
    return x


def passed_along(x, axis, by):
    size = lax.axis_size(axis)
    pairs = [(i, i + by) for i in range(size) if 0 <= i + by < size]
    return lax.ppermute(x, axis, pairs)


def band_matrix(taps, out_rows, in_cols):
    period = in_cols + 5
    padded = jnp.pad(taps, (0, period - taps.shape[0]))
    return jnp.tile(padded, out_rows)[: out_rows * in_cols].reshape(out_rows, in_cols)


def whiten(block):
    length, channels = block.shape
    bins = length // 16
    freqs = jnp.arange(1, bins + 1, dtype=jnp.int32)[:, None]
    times = jnp.arange(length, dtype=jnp.int32)[None, :]
    angle = (freqs * times % length).astype(jnp.float32) * (2.0 * math.pi / length)
    table = jnp.concatenate([jnp.cos(angle), -jnp.sin(angle)], axis=0)
    table_high = table.astype(jnp.bfloat16)
    table_low = (table - table_high.astype(jnp.float32)).astype(jnp.bfloat16)
    spectrum = jnp.dot(table_high, block, preferred_element_type=jnp.float32)
    spectrum = spectrum + jnp.dot(table_low, block, preferred_element_type=jnp.float32)
    squares = spectrum * spectrum
    power = jnp.sum(squares[:bins] + squares[bins:], axis=1) / (2 * channels)
    gain = lax.rsqrt(power + 1e-06)
    return (spectrum * jnp.concatenate([gain, gain])[:, None]).astype(jnp.bfloat16)


def cross_tile(mine, partner, scale):
    product = lax.dot_general(
        mine, partner, (((0,), (0,)), ((), ())), preferred_element_type=jnp.float32
    )
    return product * scale


def streamed(raw, taps, tile_dist, tile_count, owner):
    rows = raw.shape[0]
    width = taps.shape[0]
    half = (width - 1) // 2
    out_rows = rows // 5
    banded = band_matrix(taps, out_rows, rows + 2 * half)
    padded = extended(raw, (("chan", 0),), half)
    filtered = jnp.dot(banded, padded, preferred_element_type=jnp.float32)
    decimated = filtered.astype(jnp.bfloat16)
    regrouped = lax.all_to_all(decimated, "chan", split_axis=1, concat_axis=0, tiled=True)
    whitened = whiten(regrouped)
    channels = whitened.shape[1]
    scale = 1.0 / whitened.shape[0]
    bands = tile_dist.shape[1]
    slots = jnp.arange(bands, dtype=jnp.int32) < tile_count[0]
    stacks = []
    for distance in range(1, bands + 1):
        partner = passed_along(whitened, "chan", -distance)
        listed = jnp.sum(((tile_dist[0] == distance) & slots).astype(jnp.int32))
        tile = lax.cond(
            listed > 0,
            lambda first, second: cross_tile(first, second, scale),
            lambda first, second: jnp.zeros((channels, channels), jnp.float32),
            whitened,
            partner,
        )
        stacks.append(tile)
    stacked = jnp.stack(stacks)
    totals = lax.psum(stacked, "chan")
    selected = (owner == lax.axis_index("chan")).astype(jnp.float32)
    return jnp.einsum("b,bxy->xy", selected, totals, precision=lax.Precision.HIGHEST)[None]


def split(x):
    high = x.astype(jnp.bfloat16)
    low = (x - high.astype(jnp.float32)).astype(jnp.bfloat16)
    return high, low


def mm(a, b):
    return jnp.dot(a, b, preferred_element_type=jnp.float32)


def fused_kernel(
    n, bands, pieces,
    raw_hbm, taps_hbm, dist_hbm, count_hbm, owner_hbm, out_ref,
    raw_ref, taps_ref, dist_ref, count_ref, owner_ref, loads, smalls,
    both, pair, send1, recv1, same, cross, sent, rs0, rs1, rs2, rs3,
):
    me = lax.axis_index("chan")
    chips = n // 2
    chip, core = me // 2, me % 2
    other = chip * 2 + 1 - core
    rows, channels = raw_ref.shape
    block = channels // n
    steps = rows // 5
    length = steps * n
    bins = length // 16
    mine = 2 * bins // n
    hc = channels // 2
    width = hc // pieces
    window = 128
    lead = (window - steps) // 2
    half = (taps_hbm.shape[0] - 1) // 2
    lanes = 1024
    start = lanes - 5 * lead - half

    small = [
        pltpu.make_async_copy(source, held, smalls.at[at])
        for at, (source, held) in enumerate(
            [
                (taps_hbm, taps_ref),
                (dist_hbm, dist_ref),
                (count_hbm, count_ref),
                (owner_hbm, owner_ref),
            ]
        )
    ]
    for load in small:
        load.start()

    def load(p, h):
        cols = pl.ds(h * hc + p * width, width)
        return pltpu.make_async_copy(
            raw_hbm.at[:, cols], raw_ref.at[:, cols], loads.at[2 * p + h]
        )

    for p in range(pieces):
        for h in range(2):
            load(p, h).start()

    z, y = chip // 2, chip % 2

    def peer(k):
        far = [z, z + 1 - 2 * (z % 2), lax.rem(z + 2, 4), 3 - z][k // 2]
        return far * 2 + (1 - y if k % 2 else y)

    order = list(range(chips - 1, 0, -1))
    barrier = pltpu.get_barrier_semaphore()
    for k in order:
        pl.semaphore_signal(
            barrier, inc=1, device_id={"chan": peer(k) * 2 + core}, device_id_type=MESH
        )
    pl.semaphore_signal(barrier, inc=1, device_id={"chan": other}, device_id_type=MESH)

    row = lax.broadcasted_iota(jnp.int32, (2 * bins, window), 0)
    col = lax.broadcasted_iota(jnp.int32, (2 * bins, window), 1)
    place = row % mine
    rank = row // mine
    holder = (rank % chips) * 2 + rank // chips
    freq = holder * (mine // 2) + place % (mine // 2) + 1
    time = me * steps - lead + col
    turn = (freq * time + jnp.where(place >= mine // 2, length // 4, 0)) & (length - 1)
    table = jnp.cos(turn.astype(jnp.float32) * (2.0 * math.pi / length))
    table = jnp.where((time >= 0) & (time < length), table, 0.0)
    table_high, table_low = split(table)

    for load_one in small:
        load_one.wait()
    tap = taps_ref[...].astype(jnp.float32).reshape(1, -1)
    line = jnp.concatenate(
        [
            jnp.zeros((1, start), jnp.float32),
            tap,
            jnp.zeros((1, lanes - start - tap.shape[1]), jnp.float32),
        ],
        axis=1,
    )
    first = pltpu.roll(jnp.broadcast_to(line, (8, lanes)), 0, 1, stride=5, stride_axis=0)
    banded = jnp.concatenate(
        [pltpu.roll(first, 40 * q, 1)[:, :384] for q in range(window // 8)], axis=0
    ).astype(jnp.bfloat16)[:, :rows]
    gmap = mm(table_high, banded) + mm(table_low, banded)
    gmap = gmap.astype(jnp.bfloat16)

    lines = lax.broadcasted_iota(jnp.int32, (2 * mine, 128), 0)
    info = jnp.zeros((2 * mine, 128), jnp.float32)
    for d in range(bands):
        listed = jnp.int32(0)
        for s in range(bands):
            hit = (dist_ref[0, s] == d + 1) & (s < count_ref[0])
            listed = listed + hit.astype(jnp.int32)
        info = jnp.where(lines == core * mine + d, listed.astype(jnp.float32), info)
    both[:, :, hc:] = jnp.broadcast_to(info[None], (n, 2 * mine, 128)).astype(jnp.bfloat16)
    chosen = [(owner_ref[d] == me).astype(jnp.float32) for d in range(bands)]

    def transform(p):
        halves = []
        for h in range(2):
            load(p, h).wait()
            part = raw_ref[:, h * hc + p * width : h * hc + (p + 1) * width]
            halves.append(mm(gmap, part).reshape(n, mine, width))
        both[:, :, p * width : (p + 1) * width] = jnp.concatenate(halves, axis=1).astype(
            jnp.bfloat16
        )

    def span(p, extra=128):
        return p * width, width + (extra if p == pieces - 1 else 0)

    def remote(source, target, phase, sem, to):
        return pltpu.make_async_remote_copy(
            src_ref=source, dst_ref=target, send_sem=sent.at[phase], recv_sem=sem,
            device_id={"chan": to}, device_id_type=MESH,
        )

    def copy0(p):
        cols = pl.ds(*span(p))
        return remote(
            both.at[pl.ds((1 - core) * chips, chips), :, cols], pair.at[:, :, cols],
            0, rs0.at[p], other,
        )

    def copy1(p, k):
        cols = pl.ds(*span(p))
        return remote(
            send1.at[k, :, cols], recv1.at[k, :, cols], 1, rs1.at[p], peer(k) * 2 + core
        )

    def copy2(p, k):
        cols = pl.ds(*span(p, 0))
        return remote(
            same.at[0, :, cols], same.at[k, :, cols], 2, rs2.at[p], peer(k) * 2 + core
        )

    def copy3(p):
        cols = pl.ds(*span(p, 0))
        return remote(same.at[:, :, cols], cross.at[:, :, cols], 3, rs3.at[p], other)

    others = pl.ds(1, chips - 1)

    def arrived1(p):
        region = recv1.at[others, :, pl.ds(*span(p))]
        remote(region, region, 1, rs1.at[p], other).wait_recv()

    def arrived2(p):
        region = same.at[others, :, pl.ds(*span(p, 0))]
        remote(region, region, 2, rs2.at[p], other).wait_recv()

    for p in range(pieces):
        transform(p)
    pl.semaphore_wait(barrier, chips)
    for p in range(pieces):
        copy0(p).start()
    for p in range(pieces):
        at, size = span(p)
        cols = slice(at, at + size)
        copy0(p).wait_recv()
        for k in order:
            own = both[core * chips + peer(k), :, cols].astype(jnp.float32)
            send1[k, :, cols] = (own + pair[peer(k), :, cols].astype(jnp.float32)).astype(
                jnp.bfloat16
            )
            copy1(p, k).start()
        own = both[core * chips + chip, :, cols].astype(jnp.float32)
        recv1[0, :, cols] = (own + pair[chip, :, cols].astype(jnp.float32)).astype(jnp.bfloat16)

    for p in range(pieces):
        arrived1(p)
        cols = slice(p * width, (p + 1) * width)
        total = recv1[0, :, cols].astype(jnp.float32)
        for k in range(1, chips):
            total = total + recv1[k, :, cols].astype(jnp.float32)
        squares = total * total
        white = []
        for b in range(width // block):
            at = slice(b * block, (b + 1) * block)
            power = jnp.sum(squares[:, at], axis=1, keepdims=True)
            turned = [
                pltpu.roll(power[h * mine : (h + 1) * mine], mine // 2, 0) for h in range(2)
            ]
            power = (power + jnp.concatenate(turned, axis=0)) / (2 * block)
            white.append(total[:, at] * lax.rsqrt(power + 1e-06))
        same[0, :, cols] = jnp.concatenate(white, axis=1).astype(jnp.bfloat16)
        for k in order:
            copy2(p, k).start()

    weights = []
    for i in range(n):
        weight = jnp.zeros((1, 128), jnp.float32)
        for d in range(bands):
            at = i % 2 * mine + d
            weight = weight + recv1[peer(i // 2), at : at + 1, hc:].astype(jnp.float32) * chosen[d]
        weights.append(jnp.broadcast_to(weight, (mine, block)))
    scales = [
        jnp.concatenate([weights[t], weights[t + n // 2]], axis=0) for t in range(n // 2)
    ]

    def products(held):
        held = held.astype(jnp.float32)
        tiles = [held[:, t * block : (t + 1) * block] for t in range(n // 2)]
        left = [tiles[t] * scales[t] for t in range(n // 2)]
        for d in range(bands):
            tiles.append(
                jnp.concatenate([tiles[d][mine:], jnp.zeros((mine, block), jnp.float32)], axis=0)
            )
        right = []
        for t in range(n // 2):
            tile = tiles[t + 1] * chosen[0]
            for d in range(1, bands):
                tile = tile + tiles[t + d + 1] * chosen[d]
            right.append(tile)
        return left, right

    def add(total, refs):
        lefts, rights = [], []
        for held in refs:
            left, right = products(held)
            lefts += left
            rights += right
        left = jnp.concatenate(lefts, axis=0).astype(jnp.bfloat16)
        right = jnp.concatenate(rights, axis=0).astype(jnp.bfloat16)
        return total + lax.dot_general(
            left, right, (((0,), (0,)), ((), ())), preferred_element_type=jnp.float32
        )

    for p in range(pieces):
        arrived2(p)
        copy3(p).start()
    result = jnp.zeros((block, block), jnp.float32)
    for k in range(0, chips, 2):
        result = add(result, [same[k], same[k + 1]])
    for p in range(pieces):
        copy3(p).wait_recv()
    for k in range(0, chips, 2):
        result = add(result, [cross[k], cross[k + 1]])
    out_ref[0] = result * (1.0 / (2 * bins))

    remote(pair, pair, 0, rs0.at[0], other).wait_send()
    remote(recv1.at[others], recv1.at[others], 1, rs0.at[0], other).wait_send()
    remote(same.at[others], same.at[others], 2, rs0.at[0], other).wait_send()
    remote(same, same, 3, rs0.at[0], other).wait_send()


def fused(raw, taps, tile_dist, tile_count, owner):
    n = lax.axis_size("chan")
    rows, channels = raw.shape
    bands = tile_dist.shape[1]
    block = channels // n
    steps = rows // 5
    mine = 2 * (steps * n // 16) // n
    chips = n // 2
    hc = channels // 2
    pieces = 4
    vmem, hbm = pl.BlockSpec(memory_space=pltpu.VMEM), pl.BlockSpec(memory_space=pltpu.HBM)
    dma = pltpu.SemaphoreType.DMA
    held = functools.partial(pltpu.with_memory_space_constraint, memory_space=pltpu.HBM)
    return pl.pallas_call(
        functools.partial(fused_kernel, n, bands, pieces),
        out_shape=jax.ShapeDtypeStruct((1, block, block), jnp.float32),
        in_specs=[hbm] * 5,
        out_specs=vmem,
        scratch_shapes=[
            pltpu.VMEM(raw.shape, raw.dtype),
            pltpu.VMEM(taps.shape, taps.dtype),
            pltpu.SMEM(tile_dist.shape, jnp.int32),
            pltpu.SMEM(tile_count.shape, jnp.int32),
            pltpu.SMEM(owner.shape, jnp.int32),
            dma((2 * pieces,)),
            dma((4,)),
            pltpu.VMEM((n, 2 * mine, hc + 128), jnp.bfloat16),
            pltpu.VMEM((chips, 2 * mine, hc + 128), jnp.bfloat16),
            pltpu.VMEM((chips, 2 * mine, hc + 128), jnp.bfloat16),
            pltpu.VMEM((chips, 2 * mine, hc + 128), jnp.bfloat16),
            pltpu.VMEM((chips, 2 * mine, hc), jnp.bfloat16),
            pltpu.VMEM((chips, 2 * mine, hc), jnp.bfloat16),
            dma((4,)),
            dma((pieces,)),
            dma((pieces,)),
            dma((pieces,)),
            dma((pieces,)),
        ],
        compiler_params=pltpu.CompilerParams(
            collective_id=0, has_side_effects=True, vmem_limit_bytes=int(53.25 * 2**20)
        ),
    )(held(raw), held(taps), held(tile_dist), tile_count, held(owner))


def shards(raw, taps, tile_dist, tile_count, owner):
    n = lax.axis_size("chan")
    rows, channels = raw.shape
    steps = rows // 5
    fits = (
        channels == 128 * n
        and n == 16
        and rows == 320
        and taps.shape[0] == 255
        and tile_dist.shape[1] == 4
    )
    path = fused if fits else streamed
    return path(raw, taps, tile_dist, tile_count, owner)


def solution(mesh):
    in_specs = (P("chan", "groups"), P(), P("chan", "groups"), P(("groups", "chan")), P("groups"))
    out_specs = P("chan", "groups", None)
    return jax.shard_map(shards, mesh=mesh, in_specs=in_specs, out_specs=out_specs, check_vma=False)
```

```python
import functools
import math

import jax
import jax.numpy as jnp
from jax import lax
from jax.experimental import pallas as pl
from jax.experimental.pallas import tpu as pltpu
from jax.sharding import PartitionSpec as P

MESH = pl.DeviceIdType.MESH


def extended(x, sides, width):
    for axis, dim in sides:
        size, length = (lax.axis_size(axis), x.shape[dim])
        up = [(i, (i + 1) % size) for i in range(size - 1)]
        down = [(j, i) for i, j in up]
        last = lax.slice_in_dim(x, length - width, length, axis=dim)
        initial = lax.slice_in_dim(x, 0, width, axis=dim)
        before = lax.ppermute(last, axis, up)
        after = lax.ppermute(initial, axis, down)
        x = jnp.concatenate([before, x, after], axis=dim)
    return x


def passed_along(x, axis, by):
    size = lax.axis_size(axis)
    pairs = [(i, i + by) for i in range(size) if 0 <= i + by < size]
    return lax.ppermute(x, axis, pairs)


def band_matrix(taps, out_rows, in_cols):
    period = in_cols + 5
    padded = jnp.pad(taps, (0, period - taps.shape[0]))
    return jnp.tile(padded, out_rows)[: out_rows * in_cols].reshape(out_rows, in_cols)


def whiten(block):
    length, channels = block.shape
    bins = length // 16
    freqs = jnp.arange(1, bins + 1, dtype=jnp.int32)[:, None]
    times = jnp.arange(length, dtype=jnp.int32)[None, :]
    angle = (freqs * times % length).astype(jnp.float32) * (2.0 * math.pi / length)
    table = jnp.concatenate([jnp.cos(angle), -jnp.sin(angle)], axis=0)
    table_high = table.astype(jnp.bfloat16)
    table_low = (table - table_high.astype(jnp.float32)).astype(jnp.bfloat16)
    spectrum = jnp.dot(table_high, block, preferred_element_type=jnp.float32)
    spectrum = spectrum + jnp.dot(table_low, block, preferred_element_type=jnp.float32)
    squares = spectrum * spectrum
    power = jnp.sum(squares[:bins] + squares[bins:], axis=1) / (2 * channels)
    gain = lax.rsqrt(power + 1e-06)
    return (spectrum * jnp.concatenate([gain, gain])[:, None]).astype(jnp.bfloat16)


def cross_tile(mine, partner, scale):
    product = lax.dot_general(
        mine, partner, (((0,), (0,)), ((), ())), preferred_element_type=jnp.float32
    )
    return product * scale


def streamed(raw, taps, tile_dist, tile_count, owner):
    rows = raw.shape[0]
    width = taps.shape[0]
    half = (width - 1) // 2
    out_rows = rows // 5
    banded = band_matrix(taps, out_rows, rows + 2 * half)
    padded = extended(raw, (("chan", 0),), half)
    filtered = jnp.dot(banded, padded, preferred_element_type=jnp.float32)
    decimated = filtered.astype(jnp.bfloat16)
    regrouped = lax.all_to_all(decimated, "chan", split_axis=1, concat_axis=0, tiled=True)
    whitened = whiten(regrouped)
    channels = whitened.shape[1]
    scale = 1.0 / whitened.shape[0]
    bands = tile_dist.shape[1]
    slots = jnp.arange(bands, dtype=jnp.int32) < tile_count[0]
    stacks = []
    for distance in range(1, bands + 1):
        partner = passed_along(whitened, "chan", -distance)
        listed = jnp.sum(((tile_dist[0] == distance) & slots).astype(jnp.int32))
        tile = lax.cond(
            listed > 0,
            lambda first, second: cross_tile(first, second, scale),
            lambda first, second: jnp.zeros((channels, channels), jnp.float32),
            whitened,
            partner,
        )
        stacks.append(tile)
    stacked = jnp.stack(stacks)
    totals = lax.psum(stacked, "chan")
    selected = (owner == lax.axis_index("chan")).astype(jnp.float32)
    return jnp.einsum("b,bxy->xy", selected, totals, precision=lax.Precision.HIGHEST)[None]


def split(x):
    high = x.astype(jnp.bfloat16)
    low = (x - high.astype(jnp.float32)).astype(jnp.bfloat16)
    return high, low


def mm(a, b):
    return jnp.dot(a, b, preferred_element_type=jnp.float32)


def fused_kernel(
    n, bands, widths, cuts,
    raw_hbm, taps_hbm, dist_hbm, count_hbm, owner_hbm, out_ref,
    raw_ref, taps_ref, dist_ref, count_ref, owner_ref, loads, smalls,
    both, pair, send1, recv1, same, cross, ready, info, info_cross, sent, rs0, rs1, rs2, rs3, rs4,
):
    me = lax.axis_index("chan")
    chips = n // 2
    chip, core = me // 2, me % 2
    other = chip * 2 + 1 - core
    rows, channels = raw_ref.shape
    block = channels // n
    steps = rows // 5
    length = steps * n
    bins = length // 16
    mine = 2 * bins // n
    hc = channels // 2
    pieces = len(widths)
    starts = [sum(widths[:p]) for p in range(pieces)]
    edges = [sum(cuts[:c]) for c in range(len(cuts))]
    window = 128
    lead = (window - steps) // 2
    half = (taps_hbm.shape[0] - 1) // 2
    lanes = 1024
    start = lanes - 5 * lead - half

    z, y = chip // 2, chip % 2

    def peer(k):
        far = [z, z + 1 - 2 * (z % 2), lax.rem(z + 2, 4), 3 - z][k // 2]
        return far * 2 + (1 - y if k % 2 else y)

    order = list(range(chips - 1, 0, -1))

    def slot(to):
        low = y + to % 2 - 2 * y * (to % 2)
        mid = z % 2 + to // 2 % 2 - 2 * (z % 2) * (to // 2 % 2)
        high = z // 2 + to // 4 - 2 * (z // 2) * (to // 4)
        return 4 * high + 2 * mid + low

    def ranked(way):
        if way == "rot":
            tos = [lax.rem(chip + k, chips) for k in range(1, chips)]
        elif way == "back":
            tos = [lax.rem(chip + k, chips) for k in range(chips - 1, 0, -1)]
        elif way == "xor":
            return [(peer(k), k) for k in order]
        else:
            tos = [k + (k >= chip).astype(jnp.int32) for k in range(chips - 1)]
            if way == "down":
                tos = tos[::-1]
        return [(to, slot(to)) for to in tos]

    first_order = ranked("xor")
    second_order = ranked("up")
    barrier = pltpu.get_barrier_semaphore()

    def greet(semaphore, to):
        pl.semaphore_signal(semaphore, inc=1, device_id={"chan": to}, device_id_type=MESH)

    @pl.when(core == 1)
    def _():
        greet(barrier, other)

    for k in order:
        greet(barrier, peer(k) * 2 + 1)

    small = [
        pltpu.make_async_copy(source, held, smalls.at[at])
        for at, (source, held) in enumerate(
            [
                (taps_hbm, taps_ref),
                (dist_hbm, dist_ref),
                (count_hbm, count_ref),
                (owner_hbm, owner_ref),
            ]
        )
    ]
    for load in small:
        load.start()

    def load(p, h):
        cols = pl.ds(h * hc + edges[p], cuts[p])
        return pltpu.make_async_copy(
            raw_hbm.at[:, cols], raw_ref.at[:, cols], loads.at[2 * p + h]
        )

    for c in range(len(cuts)):
        for h in range(2):
            load(c, h).start()

    row = lax.broadcasted_iota(jnp.int32, (2 * bins, window), 0)
    col = lax.broadcasted_iota(jnp.int32, (2 * bins, window), 1)
    place = row % mine
    rank = row // mine
    holder = (rank % chips) * 2 + rank // chips
    freq = holder * (mine // 2) + place % (mine // 2) + 1
    time = me * steps - lead + col
    turn = (freq * time + jnp.where(place >= mine // 2, length // 4, 0)) & (length - 1)
    table = jnp.cos(turn.astype(jnp.float32) * (2.0 * math.pi / length))
    table = jnp.where((time >= 0) & (time < length), table, 0.0)
    table_high, table_low = split(table)

    for load_one in small:
        load_one.wait()
    tap = taps_ref[...].astype(jnp.float32).reshape(1, -1)
    line = jnp.concatenate(
        [
            jnp.zeros((1, start), jnp.float32),
            tap,
            jnp.zeros((1, lanes - start - tap.shape[1]), jnp.float32),
        ],
        axis=1,
    )
    first = pltpu.roll(jnp.broadcast_to(line, (8, lanes)), 0, 1, stride=5, stride_axis=0)
    banded = jnp.concatenate(
        [pltpu.roll(first, 40 * q, 1)[:, :384] for q in range(window // 8)], axis=0
    ).astype(jnp.bfloat16)[:, :rows]
    gmap = mm(table_high, banded) + mm(table_low, banded)
    gmap = gmap.astype(jnp.bfloat16)

    lane = lax.broadcasted_iota(jnp.int32, (1, 128), 1)
    row = jnp.zeros((1, 128), jnp.float32)
    for d in range(bands):
        listed = jnp.int32(0)
        for s in range(bands):
            hit = (dist_ref[0, s] == d + 1) & (s < count_ref[0])
            listed = listed + hit.astype(jnp.int32)
        row = jnp.where(lane == d, listed.astype(jnp.float32), row)
    info[0] = row
    chosen = [(owner_ref[d] == me).astype(jnp.float32) for d in range(bands)]

    def transform(c):
        halves = []
        for h in range(2):
            load(c, h).wait()
            at = h * hc + edges[c]
            halves.append(mm(gmap, raw_ref[:, at : at + cuts[c]]).reshape(n, mine, cuts[c]))
        both[:, :, edges[c] : edges[c] + cuts[c]] = jnp.concatenate(halves, axis=1).astype(
            jnp.bfloat16
        )

    def span(p):
        return starts[p], widths[p]

    def remote(source, target, phase, sem, to):
        return pltpu.make_async_remote_copy(
            src_ref=source, dst_ref=target, send_sem=sent.at[phase], recv_sem=sem,
            device_id={"chan": to}, device_id_type=MESH,
        )

    def copy0(c):
        cols = pl.ds(edges[c], cuts[c])
        return remote(
            both.at[pl.ds((1 - core) * chips, chips), :, cols], pair.at[:, :, cols],
            0, rs0.at[c], other,
        )

    def tell(to, k):
        return remote(info.at[0], info.at[k], 4, rs4.at[0], to * 2 + core)

    def copy1(p, to, k):
        cols = pl.ds(*span(p))
        return remote(send1.at[k, :, cols], recv1.at[k, :, cols], 1, rs1.at[p], to * 2 + core)

    def copy2(p, to, k):
        cols = pl.ds(*span(p))
        return remote(same.at[0, :, cols], same.at[k, :, cols], 2, rs2.at[p], to * 2 + core)

    def copy3(p):
        cols = pl.ds(*span(p))
        return remote(same.at[:, :, cols], cross.at[:, :, cols], 3, rs3.at[p], other)

    def pass_on():
        return remote(info, info_cross, 5, rs4.at[1], other)

    others = pl.ds(1, chips - 1)

    def arrived1(p):
        region = recv1.at[others, :, pl.ds(*span(p))]
        remote(region, region, 1, rs1.at[p], other).wait_recv()

    def arrived2(p):
        region = same.at[others, :, pl.ds(*span(p))]
        remote(region, region, 2, rs2.at[p], other).wait_recv()

    @pl.when(core == 0)
    def _():
        pl.semaphore_wait(barrier, 1)
        greet(ready, other)

    for c in range(len(cuts)):
        transform(c)
        if c == 0:

            @pl.when(core == 1)
            def _():
                pl.semaphore_wait(ready, 1)

        copy0(c).start()

    @pl.when(core == 1)
    def _():
        pl.semaphore_wait(barrier, 2 * (chips - 1))
        greet(ready, other)

    @pl.when(core == 0)
    def _():
        pl.semaphore_wait(ready, 1)

    for to, k in first_order:
        tell(to, k).start()
    for p in range(pieces):
        at, size = span(p)
        cols = slice(at, at + size)
        for c in range(len(cuts)):
            if at <= edges[c] < at + size:
                copy0(c).wait_recv()
        for to, k in first_order:
            own = both[core * chips + to, :, cols].astype(jnp.float32)
            send1[k, :, cols] = (own + pair[to, :, cols].astype(jnp.float32)).astype(jnp.bfloat16)
            copy1(p, to, k).start()
        own = both[core * chips + chip, :, cols].astype(jnp.float32)
        recv1[0, :, cols] = (own + pair[chip, :, cols].astype(jnp.float32)).astype(jnp.bfloat16)

    for p in range(pieces):
        arrived1(p)
        cols = slice(starts[p], starts[p] + widths[p])
        total = recv1[0, :, cols].astype(jnp.float32)
        for k in range(1, chips):
            total = total + recv1[k, :, cols].astype(jnp.float32)
        squares = total * total
        white = []
        for b in range(widths[p] // block):
            at = slice(b * block, (b + 1) * block)
            power = jnp.sum(squares[:, at], axis=1, keepdims=True)
            turned = [
                pltpu.roll(power[h * mine : (h + 1) * mine], mine // 2, 0) for h in range(2)
            ]
            power = (power + jnp.concatenate(turned, axis=0)) / (2 * block)
            white.append(total[:, at] * lax.rsqrt(power + 1e-06))
        same[0, :, cols] = jnp.concatenate(white, axis=1).astype(jnp.bfloat16)
        for to, k in second_order:
            copy2(p, to, k).start()

    remote(info.at[others], info.at[others], 4, rs4.at[0], other).wait_recv()
    pass_on().start()
    pass_on().wait_recv()
    weights = []
    for i in range(n):
        here = (i % 2 == core).astype(jnp.float32)
        line = info[peer(i // 2)] * here + info_cross[peer(i // 2)] * (1.0 - here)
        weight = jnp.zeros((1, 1), jnp.float32)
        for d in range(bands):
            weight = weight + line[:, d : d + 1] * chosen[d]
        weights.append(jnp.broadcast_to(weight, (mine, block)))
    scales = [
        jnp.concatenate([weights[t], weights[t + n // 2]], axis=0) for t in range(n // 2)
    ]

    scales = [scale.astype(jnp.bfloat16) for scale in scales]
    picks = [jnp.full((2 * mine, block), pick, jnp.float32).astype(jnp.bfloat16) for pick in chosen]

    def add(total, held):
        lefts, rights = [], []
        for k in range(chips):
            tiles = [held[k, :, t * block : (t + 1) * block] for t in range(n // 2)]
            lefts += [tiles[t] * scales[t] for t in range(n // 2)]
            for d in range(bands):
                later = tiles[d].astype(jnp.float32)[mine:]
                tiles.append(
                    jnp.concatenate([later, jnp.zeros_like(later)], axis=0).astype(jnp.bfloat16)
                )
            for t in range(n // 2):
                tile = tiles[t + 1] * picks[0]
                for d in range(1, bands):
                    tile = tile + tiles[t + d + 1] * picks[d]
                rights.append(tile)
        left = jnp.concatenate(lefts, axis=0)
        right = jnp.concatenate(rights, axis=0)
        return total + lax.dot_general(
            left, right, (((0,), (0,)), ((), ())), preferred_element_type=jnp.float32
        )

    for p in range(pieces):
        arrived2(p)
        copy3(p).start()
    result = add(jnp.zeros((block, block), jnp.float32), same)
    for p in range(pieces):
        copy3(p).wait_recv()
    result = add(result, cross)
    out_ref[0] = result * (1.0 / (2 * bins))

    remote(pair, pair, 0, rs0.at[0], other).wait_send()
    remote(recv1.at[others], recv1.at[others], 1, rs0.at[0], other).wait_send()
    remote(same.at[others], same.at[others], 2, rs0.at[0], other).wait_send()
    remote(same, same, 3, rs0.at[0], other).wait_send()
    remote(info.at[others], info.at[others], 4, rs0.at[0], other).wait_send()
    remote(info, info, 5, rs0.at[0], other).wait_send()


def fused(raw, taps, tile_dist, tile_count, owner):
    n = lax.axis_size("chan")
    rows, channels = raw.shape
    bands = tile_dist.shape[1]
    block = channels // n
    steps = rows // 5
    mine = 2 * (steps * n // 16) // n
    chips = n // 2
    hc = channels // 2
    widths = [hc * k // 8 for k in (4,4,)]
    cuts = [hc * k // 8 for k in (4,4,)]
    pieces = len(widths)
    vmem, hbm = pl.BlockSpec(memory_space=pltpu.VMEM), pl.BlockSpec(memory_space=pltpu.HBM)
    dma = pltpu.SemaphoreType.DMA
    held = functools.partial(pltpu.with_memory_space_constraint, memory_space=pltpu.HBM)
    return pl.pallas_call(
        functools.partial(fused_kernel, n, bands, widths, cuts),
        out_shape=jax.ShapeDtypeStruct((1, block, block), jnp.float32),
        in_specs=[hbm] * 5,
        out_specs=vmem,
        scratch_shapes=[
            pltpu.VMEM(raw.shape, raw.dtype),
            pltpu.VMEM(taps.shape, taps.dtype),
            pltpu.SMEM(tile_dist.shape, jnp.int32),
            pltpu.SMEM(tile_count.shape, jnp.int32),
            pltpu.SMEM(owner.shape, jnp.int32),
            dma((2 * len(cuts),)),
            dma((4,)),
            pltpu.VMEM((n, 2 * mine, hc), jnp.bfloat16),
            pltpu.VMEM((chips, 2 * mine, hc), jnp.bfloat16),
            pltpu.VMEM((chips, 2 * mine, hc), jnp.bfloat16),
            pltpu.VMEM((chips, 2 * mine, hc), jnp.bfloat16),
            pltpu.VMEM((chips, 2 * mine, hc), jnp.bfloat16),
            pltpu.VMEM((chips, 2 * mine, hc), jnp.bfloat16),
            pltpu.SemaphoreType.REGULAR,
            pltpu.VMEM((chips, 1, 128), jnp.float32),
            pltpu.VMEM((chips, 1, 128), jnp.float32),
            dma((6,)),
            dma((len(cuts),)),
            dma((pieces,)),
            dma((pieces,)),
            dma((pieces,)),
            dma((2,)),
        ],
        compiler_params=pltpu.CompilerParams(
            collective_id=0, has_side_effects=True, vmem_limit_bytes=int(53.25 * 2**20)
        ),
    )(held(raw), held(taps), held(tile_dist), tile_count, held(owner))


def shards(raw, taps, tile_dist, tile_count, owner):
    n = lax.axis_size("chan")
    rows, channels = raw.shape
    steps = rows // 5
    fits = (
        channels == 128 * n
        and n == 16
        and rows == 320
        and taps.shape[0] == 255
        and tile_dist.shape[1] == 4
    )
    path = fused if fits else streamed
    return path(raw, taps, tile_dist, tile_count, owner)


def solution(mesh):
    in_specs = (P("chan", "groups"), P(), P("chan", "groups"), P(("groups", "chan")), P("groups"))
    out_specs = P("chan", "groups", None)
    return jax.shard_map(shards, mesh=mesh, in_specs=in_specs, out_specs=out_specs, check_vma=False)
```

```python
import functools
import math

import jax
import jax.numpy as jnp
from jax import lax
from jax.experimental import pallas as pl
from jax.experimental.pallas import tpu as pltpu
from jax.sharding import PartitionSpec as P
import numpy as np

MESH = pl.DeviceIdType.MESH


def extended(x, sides, width):
    for axis, dim in sides:
        size, length = (lax.axis_size(axis), x.shape[dim])
        up = [(i, (i + 1) % size) for i in range(size - 1)]
        down = [(j, i) for i, j in up]
        last = lax.slice_in_dim(x, length - width, length, axis=dim)
        initial = lax.slice_in_dim(x, 0, width, axis=dim)
        before = lax.ppermute(last, axis, up)
        after = lax.ppermute(initial, axis, down)
        x = jnp.concatenate([before, x, after], axis=dim)
    return x


def passed_along(x, axis, by):
    size = lax.axis_size(axis)
    pairs = [(i, i + by) for i in range(size) if 0 <= i + by < size]
    return lax.ppermute(x, axis, pairs)


def band_matrix(taps, out_rows, in_cols):
    period = in_cols + 5
    padded = jnp.pad(taps, (0, period - taps.shape[0]))
    return jnp.tile(padded, out_rows)[: out_rows * in_cols].reshape(out_rows, in_cols)


def whiten(block):
    length, channels = block.shape
    bins = length // 16
    freqs = jnp.arange(1, bins + 1, dtype=jnp.int32)[:, None]
    times = jnp.arange(length, dtype=jnp.int32)[None, :]
    angle = (freqs * times % length).astype(jnp.float32) * (2.0 * math.pi / length)
    table = jnp.concatenate([jnp.cos(angle), -jnp.sin(angle)], axis=0)
    table_high = table.astype(jnp.bfloat16)
    table_low = (table - table_high.astype(jnp.float32)).astype(jnp.bfloat16)
    spectrum = jnp.dot(table_high, block, preferred_element_type=jnp.float32)
    spectrum = spectrum + jnp.dot(table_low, block, preferred_element_type=jnp.float32)
    squares = spectrum * spectrum
    power = jnp.sum(squares[:bins] + squares[bins:], axis=1) / (2 * channels)
    gain = lax.rsqrt(power + 1e-06)
    return (spectrum * jnp.concatenate([gain, gain])[:, None]).astype(jnp.bfloat16)


def cross_tile(mine, partner, scale):
    product = lax.dot_general(
        mine, partner, (((0,), (0,)), ((), ())), preferred_element_type=jnp.float32
    )
    return product * scale


def streamed(raw, taps, tile_dist, tile_count, owner):
    rows = raw.shape[0]
    width = taps.shape[0]
    half = (width - 1) // 2
    out_rows = rows // 5
    banded = band_matrix(taps, out_rows, rows + 2 * half)
    padded = extended(raw, (("chan", 0),), half)
    filtered = jnp.dot(banded, padded, preferred_element_type=jnp.float32)
    decimated = filtered.astype(jnp.bfloat16)
    regrouped = lax.all_to_all(decimated, "chan", split_axis=1, concat_axis=0, tiled=True)
    whitened = whiten(regrouped)
    channels = whitened.shape[1]
    scale = 1.0 / whitened.shape[0]
    bands = tile_dist.shape[1]
    slots = jnp.arange(bands, dtype=jnp.int32) < tile_count[0]
    stacks = []
    for distance in range(1, bands + 1):
        partner = passed_along(whitened, "chan", -distance)
        listed = jnp.sum(((tile_dist[0] == distance) & slots).astype(jnp.int32))
        tile = lax.cond(
            listed > 0,
            lambda first, second: cross_tile(first, second, scale),
            lambda first, second: jnp.zeros((channels, channels), jnp.float32),
            whitened,
            partner,
        )
        stacks.append(tile)
    stacked = jnp.stack(stacks)
    totals = lax.psum(stacked, "chan")
    selected = (owner == lax.axis_index("chan")).astype(jnp.float32)
    return jnp.einsum("b,bxy->xy", selected, totals, precision=lax.Precision.HIGHEST)[None]


def split(x):
    high = x.astype(jnp.bfloat16)
    low = (x - high.astype(jnp.float32)).astype(jnp.bfloat16)
    return high, low


def mm(a, b):
    return jnp.dot(a, b, preferred_element_type=jnp.float32)


def window_factors(steps, lead, length, bins, reach, rank):
    width = 2 * steps + 2 * lead
    chips = length // (2 * steps)
    freq = np.arange(1, bins + 1)[:, None]
    low, high = -(reach // 5), 2 * steps + (reach - 1) // 5 + 1
    time = np.arange(low, high)[None, :]

    def table(chip):
        angle = 2.0 * np.pi * ((freq * (time + 2 * steps * chip)) % length) / length
        return np.concatenate([np.cos(angle), -np.sin(angle)], axis=0)

    basis = np.linalg.svd(table(0), full_matrices=False)[2][:rank]
    lefts = np.stack([basis @ table(chip).T for chip in range(chips)])
    padded = np.zeros((rank, width))
    padded[:, lead + low : lead + high] = basis
    rights = np.stack([padded[:, c * steps : (c + 1) * steps + 2 * lead] for c in range(2)])
    return lefts.astype(np.float32), rights.astype(np.float32)


def fused_kernel(
    n, bands,
    raw_hbm, taps_hbm, dist_hbm, count_hbm, owner_hbm, left_hbm, right_hbm, out_ref,
    raw_ref, taps_ref, dist_ref, count_ref, owner_ref, left_ref, right_ref, loads, smalls,
    joined, both, pair, send1, recv1, gath, ready, info, info_cross, sent, rs0, rs1, rs2, rs3, rs4,
):
    me = lax.axis_index("chan")
    chips = n // 2
    chip, core = me // 2, me % 2
    other = chip * 2 + 1 - core
    rows, channels = raw_ref.shape
    rank = right_ref.shape[0]
    block = channels // n
    steps = rows // 5
    length = steps * n
    bins = length // 16
    window = right_ref.shape[1]
    lead = (window - steps) // 2
    half = (taps_hbm.shape[0] - 1) // 2
    lanes = 1024
    start = lanes - 5 * lead - half
    cuts = 2
    cut = channels // cuts

    z, y = chip // 2, chip % 2

    def peer(k):
        far = [z, z + 1 - 2 * (z % 2), lax.rem(z + 2, 4), 3 - z][k // 2]
        return far * 2 + (1 - y if k % 2 else y)

    def slot(to):
        low = y + to % 2 - 2 * y * (to % 2)
        mid = z % 2 + to // 2 % 2 - 2 * (z % 2) * (to // 2 % 2)
        high = z // 2 + to // 4 - 2 * (z // 2) * (to // 4)
        return 4 * high + 2 * mid + low

    first_order = [(peer(k), k) for k in (7, 6, 5, 4, 3, 2, 1)]
    rising = [k + (k >= chip).astype(jnp.int32) for k in range(chips - 1)]
    second_order = [(to, slot(to)) for to in rising]

    barrier = pltpu.get_barrier_semaphore()

    def greet(semaphore, to):
        pl.semaphore_signal(semaphore, inc=1, device_id={"chan": to}, device_id_type=MESH)

    @pl.when(core == 1)
    def _():
        greet(barrier, other)

    for k in range(chips - 1, 0, -1):
        greet(barrier, peer(k) * 2 + 1)

    small = [
        pltpu.make_async_copy(source, held, smalls.at[at])
        for at, (source, held) in enumerate(
            [
                (taps_hbm, taps_ref),
                (right_hbm.at[core], right_ref),
                (dist_hbm, dist_ref),
                (count_hbm, count_ref),
                (owner_hbm, owner_ref),
                (left_hbm, left_ref),
            ]
        )
    ]
    for load in small[:2]:
        load.start()

    def load(c):
        cols = pl.ds(c * cut, cut)
        return pltpu.make_async_copy(raw_hbm.at[:, cols], raw_ref.at[:, cols], loads.at[c])

    for c in range(cuts):
        load(c).start()
    for load_one in small[2:]:
        load_one.start()

    for load_one in small[:2]:
        load_one.wait()
    tap = taps_ref[...].astype(jnp.float32).reshape(1, -1)
    line = jnp.concatenate(
        [
            jnp.zeros((1, start), jnp.float32),
            tap,
            jnp.zeros((1, lanes - start - tap.shape[1]), jnp.float32),
        ],
        axis=1,
    )
    first = pltpu.roll(jnp.broadcast_to(line, (8, lanes)), 0, 1, stride=5, stride_axis=0)
    banded = jnp.concatenate(
        [pltpu.roll(first, 40 * q, 1)[:, :384] for q in range(window // 8)], axis=0
    ).astype(jnp.bfloat16)[:, :rows]
    time = me * steps - lead + lax.broadcasted_iota(jnp.int32, (rank, window), 1)
    table = jnp.where((time >= 0) & (time < length), right_ref[...], 0.0)
    table_high, table_low = split(table)
    gmap = (mm(table_high, banded) + mm(table_low, banded)).astype(jnp.bfloat16)

    def transform(c):
        load(c).wait()
        part = mm(gmap, raw_ref[:, c * cut : (c + 1) * cut]).astype(jnp.bfloat16)
        for j in range(cut // block):
            at = c * (cut // block) + j
            both[at % 2 * chips + at // 2] = part[:, j * block : (j + 1) * block]

    def remote(source, target, phase, sem, to):
        return pltpu.make_async_remote_copy(
            src_ref=source, dst_ref=target, send_sem=sent.at[phase], recv_sem=sem,
            device_id={"chan": to}, device_id_type=MESH,
        )

    def copy0(c):
        few = chips // cuts
        return remote(
            both.at[pl.ds((1 - core) * chips + c * few, few)], pair.at[pl.ds(c * few, few)],
            0, rs0.at[c], other,
        )

    def tell(to, k):
        return remote(info.at[0], info.at[k], 4, rs4.at[0], to * 2 + core)

    def pass_on():
        return remote(info, info_cross, 5, rs4.at[1], other)

    def copy1(to, k):
        return remote(send1.at[k], recv1.at[k], 1, rs1, to * 2 + core)

    groups = [(0, chips // 2), (chips // 2, chips)]

    def copy2(to, k, g):
        return remote(gath.at[0, 0], gath.at[0, k], 2, rs2.at[g], to * 2 + core)

    def copy3(g):
        first, last = groups[g]
        some = pl.ds(first, last - first)
        return remote(gath.at[0, some], gath.at[1, some], 3, rs3.at[g], other)

    others = pl.ds(1, chips - 1)

    @pl.when(core == 0)
    def _():
        pl.semaphore_wait(barrier, 1)
        greet(ready, other)

    for c in range(cuts):
        transform(c)
        if c == 0:

            @pl.when(core == 1)
            def _():
                pl.semaphore_wait(ready, 1)

        copy0(c).start()

    for load_one in small[2:]:
        load_one.wait()
    lane = lax.broadcasted_iota(jnp.int32, (1, 128), 1)
    row = jnp.zeros((1, 128), jnp.float32)
    for d in range(bands):
        listed = jnp.int32(0)
        for s in range(bands):
            hit = (dist_ref[0, s] == d + 1) & (s < count_ref[0])
            listed = listed + hit.astype(jnp.int32)
        row = jnp.where(lane == d, listed.astype(jnp.float32), row)
    info[0] = row
    chosen = [(owner_ref[d] == me).astype(jnp.int32) for d in range(bands)]
    shift = sum((d + 1) * chosen[d] for d in range(bands))
    joined[...] = jnp.transpose(
        jnp.concatenate([left_ref[peer(k)] for k in range(chips)], axis=0)
    ).astype(jnp.bfloat16)

    @pl.when(core == 1)
    def _():
        pl.semaphore_wait(barrier, 2 * (chips - 1))
        greet(ready, other)

    @pl.when(core == 0)
    def _():
        pl.semaphore_wait(ready, 1)

    for c in range(cuts):
        copy0(c).wait_recv()
    for to, k in first_order:
        own = both[core * chips + to].astype(jnp.float32)
        send1[k] = (own + pair[to].astype(jnp.float32)).astype(jnp.bfloat16)
        copy1(to, k).start()
    own = both[core * chips + chip].astype(jnp.float32)
    recv1[0] = (own + pair[chip].astype(jnp.float32)).astype(jnp.bfloat16)
    for to, k in first_order:
        tell(to, k).start()

    remote(recv1.at[others], recv1.at[others], 1, rs1, other).wait_recv()
    spectrum = mm(joined[...], recv1[...].reshape(chips * rank, block))
    power = jnp.sum(spectrum * spectrum, axis=1, keepdims=True)
    power = (power[:bins] + power[bins:]) / (2 * block)
    gain = lax.rsqrt(power + 1e-06)
    gath[0, 0] = (spectrum * jnp.concatenate([gain, gain], axis=0)).astype(jnp.bfloat16)
    for to, k in second_order:
        copy2(to, k, k // (chips // 2)).start()

    remote(info.at[others], info.at[others], 4, rs4.at[0], other).wait_recv()
    pass_on().start()
    pass_on().wait_recv()
    weights = []
    for i in range(n):
        here = ((i + core) % 2 == 0).astype(jnp.float32)
        line = info[peer(i // 2)] * here + info_cross[peer(i // 2)] * (1.0 - here)
        weight = jnp.zeros((1, 1), jnp.float32)
        for d in range(bands):
            weight = weight + line[:, d : d + 1] * chosen[d].astype(jnp.float32)
        weights.append(jnp.broadcast_to(weight, (block, block)).astype(jnp.bfloat16))

    for g, (first, last) in enumerate(groups):
        low = max(first, 1)
        if last > low:
            some = gath.at[0, pl.ds(low, last - low)]
            remote(some, some, 2, rs2.at[g], other).wait_recv()
        copy3(g).start()
    for g in range(len(groups)):
        copy3(g).wait_recv()
    lefts, rights = [], []
    for i in range(n - 1):
        lefts.append(gath[(i + core) % 2, slot(i // 2)] * weights[i])
        later = jnp.minimum(i + shift, n - 1)
        rights.append(gath[(later + core) % 2, slot(later // 2)])
    result = lax.dot_general(
        jnp.concatenate(lefts, axis=0), jnp.concatenate(rights, axis=0),
        (((0,), (0,)), ((), ())), preferred_element_type=jnp.float32,
    )
    out_ref[0] = result * (1.0 / (2 * bins))

    remote(pair, pair, 0, rs0.at[0], other).wait_send()
    remote(recv1.at[others], recv1.at[others], 1, rs0.at[0], other).wait_send()
    remote(gath.at[0, others], gath.at[0, others], 2, rs0.at[0], other).wait_send()
    remote(gath.at[0], gath.at[0], 3, rs0.at[0], other).wait_send()
    remote(info.at[others], info.at[others], 4, rs0.at[0], other).wait_send()
    remote(info, info, 5, rs0.at[0], other).wait_send()


def fused(raw, taps, tile_dist, tile_count, owner):
    n = lax.axis_size("chan")
    rows, channels = raw.shape
    bands = tile_dist.shape[1]
    block = channels // n
    steps = rows // 5
    chips = n // 2
    rank = 48
    lead = (128 - steps) // 2
    lefts, rights = window_factors(
        steps, lead, steps * n, steps * n // 16, (taps.shape[0] - 1) // 2, rank
    )
    vmem, hbm = pl.BlockSpec(memory_space=pltpu.VMEM), pl.BlockSpec(memory_space=pltpu.HBM)
    dma = pltpu.SemaphoreType.DMA
    held = functools.partial(pltpu.with_memory_space_constraint, memory_space=pltpu.HBM)
    return pl.pallas_call(
        functools.partial(fused_kernel, n, bands),
        out_shape=jax.ShapeDtypeStruct((1, block, block), jnp.float32),
        in_specs=[hbm] * 7,
        out_specs=vmem,
        scratch_shapes=[
            pltpu.VMEM(raw.shape, raw.dtype),
            pltpu.VMEM(taps.shape, taps.dtype),
            pltpu.SMEM(tile_dist.shape, jnp.int32),
            pltpu.SMEM(tile_count.shape, jnp.int32),
            pltpu.SMEM(owner.shape, jnp.int32),
            pltpu.VMEM(lefts.shape, jnp.float32),
            pltpu.VMEM(rights.shape[1:], jnp.float32),
            dma((2,)),
            dma((6,)),
            pltpu.VMEM((lefts.shape[2], chips * rank), jnp.bfloat16),
            pltpu.VMEM((n, rank, block), jnp.bfloat16),
            pltpu.VMEM((chips, rank, block), jnp.bfloat16),
            pltpu.VMEM((chips, rank, block), jnp.bfloat16),
            pltpu.VMEM((chips, rank, block), jnp.bfloat16),
            pltpu.VMEM((2, chips, block, block), jnp.bfloat16),
            pltpu.SemaphoreType.REGULAR,
            pltpu.VMEM((chips, 1, 128), jnp.float32),
            pltpu.VMEM((chips, 1, 128), jnp.float32),
            dma((6,)),
            dma((2,)),
            dma,
            dma((2,)),
            dma((2,)),
            dma((2,)),
        ],
        compiler_params=pltpu.CompilerParams(
            collective_id=0, has_side_effects=True, vmem_limit_bytes=int(53.25 * 2**20)
        ),
    )(held(raw), held(taps), held(tile_dist), tile_count, held(owner), held(jnp.asarray(lefts)), held(jnp.asarray(rights)))


def shards(raw, taps, tile_dist, tile_count, owner):
    n = lax.axis_size("chan")
    rows, channels = raw.shape
    steps = rows // 5
    fits = (
        channels == 128 * n
        and n == 16
        and rows == 320
        and taps.shape[0] == 255
        and tile_dist.shape[1] == 4
    )
    path = fused if fits else streamed
    return path(raw, taps, tile_dist, tile_count, owner)


def solution(mesh):
    in_specs = (P("chan", "groups"), P(), P("chan", "groups"), P(("groups", "chan")), P("groups"))
    out_specs = P("chan", "groups", None)
    return jax.shard_map(shards, mesh=mesh, in_specs=in_specs, out_specs=out_specs, check_vma=False)
```

```python
import functools
import math

import jax
import jax.numpy as jnp
from jax import lax
from jax.experimental import pallas as pl
from jax.experimental.pallas import tpu as pltpu
from jax.sharding import PartitionSpec as P
import numpy as np

MESH = pl.DeviceIdType.MESH


def extended(x, sides, width):
    for axis, dim in sides:
        size, length = (lax.axis_size(axis), x.shape[dim])
        up = [(i, (i + 1) % size) for i in range(size - 1)]
        down = [(j, i) for i, j in up]
        last = lax.slice_in_dim(x, length - width, length, axis=dim)
        initial = lax.slice_in_dim(x, 0, width, axis=dim)
        before = lax.ppermute(last, axis, up)
        after = lax.ppermute(initial, axis, down)
        x = jnp.concatenate([before, x, after], axis=dim)
    return x


def passed_along(x, axis, by):
    size = lax.axis_size(axis)
    pairs = [(i, i + by) for i in range(size) if 0 <= i + by < size]
    return lax.ppermute(x, axis, pairs)


def band_matrix(taps, out_rows, in_cols):
    period = in_cols + 5
    padded = jnp.pad(taps, (0, period - taps.shape[0]))
    return jnp.tile(padded, out_rows)[: out_rows * in_cols].reshape(out_rows, in_cols)


def whiten(block):
    length, channels = block.shape
    bins = length // 16
    freqs = jnp.arange(1, bins + 1, dtype=jnp.int32)[:, None]
    times = jnp.arange(length, dtype=jnp.int32)[None, :]
    angle = (freqs * times % length).astype(jnp.float32) * (2.0 * math.pi / length)
    table = jnp.concatenate([jnp.cos(angle), -jnp.sin(angle)], axis=0)
    table_high = table.astype(jnp.bfloat16)
    table_low = (table - table_high.astype(jnp.float32)).astype(jnp.bfloat16)
    spectrum = jnp.dot(table_high, block, preferred_element_type=jnp.float32)
    spectrum = spectrum + jnp.dot(table_low, block, preferred_element_type=jnp.float32)
    squares = spectrum * spectrum
    power = jnp.sum(squares[:bins] + squares[bins:], axis=1) / (2 * channels)
    gain = lax.rsqrt(power + 1e-06)
    return (spectrum * jnp.concatenate([gain, gain])[:, None]).astype(jnp.bfloat16)


def cross_tile(mine, partner, scale):
    product = lax.dot_general(
        mine, partner, (((0,), (0,)), ((), ())), preferred_element_type=jnp.float32
    )
    return product * scale


def streamed(raw, taps, tile_dist, tile_count, owner):
    rows = raw.shape[0]
    width = taps.shape[0]
    half = (width - 1) // 2
    out_rows = rows // 5
    banded = band_matrix(taps, out_rows, rows + 2 * half)
    padded = extended(raw, (("chan", 0),), half)
    filtered = jnp.dot(banded, padded, preferred_element_type=jnp.float32)
    decimated = filtered.astype(jnp.bfloat16)
    regrouped = lax.all_to_all(decimated, "chan", split_axis=1, concat_axis=0, tiled=True)
    whitened = whiten(regrouped)
    channels = whitened.shape[1]
    scale = 1.0 / whitened.shape[0]
    bands = tile_dist.shape[1]
    slots = jnp.arange(bands, dtype=jnp.int32) < tile_count[0]
    stacks = []
    for distance in range(1, bands + 1):
        partner = passed_along(whitened, "chan", -distance)
        listed = jnp.sum(((tile_dist[0] == distance) & slots).astype(jnp.int32))
        tile = lax.cond(
            listed > 0,
            lambda first, second: cross_tile(first, second, scale),
            lambda first, second: jnp.zeros((channels, channels), jnp.float32),
            whitened,
            partner,
        )
        stacks.append(tile)
    stacked = jnp.stack(stacks)
    totals = lax.psum(stacked, "chan")
    selected = (owner == lax.axis_index("chan")).astype(jnp.float32)
    return jnp.einsum("b,bxy->xy", selected, totals, precision=lax.Precision.HIGHEST)[None]


def split(x):
    high = x.astype(jnp.bfloat16)
    low = (x - high.astype(jnp.float32)).astype(jnp.bfloat16)
    return high, low


def mm(a, b):
    return jnp.dot(a, b, preferred_element_type=jnp.float32)


def window_factors(steps, lead, length, bins, reach, rank):
    width = 2 * steps + 2 * lead
    chips = length // (2 * steps)
    freq = np.arange(1, bins + 1)[:, None]
    low, high = -(reach // 5), 2 * steps + (reach - 1) // 5 + 1
    time = np.arange(low, high)[None, :]

    def table(chip):
        angle = 2.0 * np.pi * ((freq * (time + 2 * steps * chip)) % length) / length
        return np.concatenate([np.cos(angle), -np.sin(angle)], axis=0)

    basis = np.linalg.svd(table(0), full_matrices=False)[2][:rank]
    lefts = np.stack([basis @ table(chip).T for chip in range(chips)])
    padded = np.zeros((rank, width))
    padded[:, lead + low : lead + high] = basis
    rights = np.stack([padded[:, c * steps : (c + 1) * steps + 2 * lead] for c in range(2)])
    return lefts.astype(np.float32), rights.astype(np.float32)


def fused_kernel(
    n, bands, kept,
    raw_hbm, taps_hbm, dist_hbm, count_hbm, owner_hbm, left_hbm, right_hbm, out_ref,
    raw_ref, taps_ref, dist_ref, count_ref, owner_ref, left_ref, right_ref, loads, smalls,
    joined, both, pair, send1, recv1, gath, turned, ready, sent, rs0, rs1, rs2, rs3,
):
    me = lax.axis_index("chan")
    chips = n // 2
    chip, core = me // 2, me % 2
    other = chip * 2 + 1 - core
    rows, channels = raw_ref.shape
    rank = right_ref.shape[0]
    block = channels // n
    steps = rows // 5
    length = steps * n
    bins = length // 16
    window = right_ref.shape[1]
    lead = (window - steps) // 2
    half = (taps_hbm.shape[0] - 1) // 2
    lanes = 1024
    start = lanes - 5 * lead - half
    cuts = 2
    cut = channels // cuts

    z, y = chip // 2, chip % 2

    def peer(k):
        far = [z, z + 1 - 2 * (z % 2), lax.rem(z + 2, 4), 3 - z][k // 2]
        return far * 2 + (1 - y if k % 2 else y)

    def slot(to):
        low = y + to % 2 - 2 * y * (to % 2)
        mid = z % 2 + to // 2 % 2 - 2 * (z % 2) * (to // 2 % 2)
        high = z // 2 + to // 4 - 2 * (z // 2) * (to // 4)
        return 4 * high + 2 * mid + low

    barrier = pltpu.get_barrier_semaphore()

    def greet(semaphore, to):
        pl.semaphore_signal(semaphore, inc=1, device_id={"chan": to}, device_id_type=MESH)

    @pl.when(core == 1)
    def _():
        greet(barrier, other)

    for q in range(chips):

        @pl.when(chip != q)
        def _():
            greet(barrier, q * 2 + 1)

    small = [
        pltpu.make_async_copy(source, held, smalls.at[at])
        for at, (source, held) in enumerate(
            [
                (taps_hbm, taps_ref),
                (right_hbm.at[core], right_ref),
                (dist_hbm, dist_ref),
                (count_hbm, count_ref),
                (owner_hbm, owner_ref),
                (left_hbm, left_ref),
            ]
        )
    ]
    for load in small[:4]:
        load.start()

    def load(c):
        cols = pl.ds(c * cut, cut)
        return pltpu.make_async_copy(raw_hbm.at[:, cols], raw_ref.at[:, cols], loads.at[c])

    for c in range(cuts):
        load(c).start()
    for load_one in small[4:]:
        load_one.start()

    for load_one in small[:2]:
        load_one.wait()
    tap = taps_ref[...].astype(jnp.float32).reshape(1, -1)
    line = jnp.concatenate(
        [
            jnp.zeros((1, start), jnp.float32),
            tap,
            jnp.zeros((1, lanes - start - tap.shape[1]), jnp.float32),
        ],
        axis=1,
    )
    first = pltpu.roll(jnp.broadcast_to(line, (8, lanes)), 0, 1, stride=5, stride_axis=0)
    banded = jnp.concatenate(
        [pltpu.roll(first, 40 * q, 1)[:, :384] for q in range(window // 8)], axis=0
    ).astype(jnp.bfloat16)[:, :rows]
    time = me * steps - lead + lax.broadcasted_iota(jnp.int32, (rank, window), 1)
    table = jnp.where((time >= 0) & (time < length), right_ref[...], 0.0)
    table_high, table_low = split(table)
    gmap = (mm(table_high, banded) + mm(table_low, banded)).astype(jnp.bfloat16)

    for load_one in small[2:4]:
        load_one.wait()
    line = lax.broadcasted_iota(jnp.int32, (rank, block), 0)
    lane = lax.broadcasted_iota(jnp.int32, (rank, block), 1)
    info = jnp.zeros((rank, block), jnp.float32)
    for d in range(bands):
        listed = jnp.int32(0)
        for s in range(bands):
            hit = (dist_ref[0, s] == d + 1) & (s < count_ref[0])
            listed = listed + hit.astype(jnp.int32)
        info = jnp.where((line == kept + core) & (lane == d), listed.astype(jnp.float32), info)

    def transform(c):
        load(c).wait()
        part = mm(gmap, raw_ref[:, c * cut : (c + 1) * cut])
        for j in range(cut // block):
            at = c * (cut // block) + j
            both[at % 2 * chips + at // 2] = (
                part[:, j * block : (j + 1) * block] + info
            ).astype(jnp.bfloat16)

    def remote(source, target, phase, sem, to):
        return pltpu.make_async_remote_copy(
            src_ref=source, dst_ref=target, send_sem=sent.at[phase], recv_sem=sem,
            device_id={"chan": to}, device_id_type=MESH,
        )

    def copy0(c):
        few = chips // cuts
        return remote(
            both.at[pl.ds((1 - core) * chips + c * few, few)], pair.at[pl.ds(c * few, few)],
            0, rs0.at[c], other,
        )

    def copy1(q):
        return remote(send1.at[q], recv1.at[slot(q)], 1, rs1, q * 2 + core)

    def copy2(source, to):
        return remote(gath.at[source], gath.at[source], 2, rs2.at[source], to * 2 + core)

    def copy3(q):
        return remote(gath.at[q], gath.at[chips + q], 3, rs3.at[q], other)

    others = pl.ds(1, chips - 1)

    @pl.when(core == 0)
    def _():
        pl.semaphore_wait(barrier, 1)
        greet(ready, other)

    for c in range(cuts):
        transform(c)
        if c == 0:

            @pl.when(core == 1)
            def _():
                pl.semaphore_wait(ready, 1)

        copy0(c).start()

    @pl.when(core == 1)
    def _():

        pl.semaphore_wait(barrier, 2 * (chips - 1))
        greet(ready, other)

    @pl.when(core == 0)
    def _():
        pl.semaphore_wait(ready, 1)

    for c in range(cuts):
        copy0(c).wait_recv()
    for q in range(chips - 1, -1, -1):
        own = both[core * chips + q].astype(jnp.float32)
        send1[q] = (own + pair[q].astype(jnp.float32)).astype(jnp.bfloat16)

        @pl.when(chip != q)
        def _():
            copy1(q).start()

    for load_one in small[4:]:
        load_one.wait()
    chosen = [(owner_ref[d] == me).astype(jnp.int32) for d in range(bands)]
    shift = sum((d + 1) * chosen[d] for d in range(bands))
    joined[...] = jnp.transpose(
        jnp.concatenate([left_ref[peer(k)] for k in range(chips)], axis=0)
    ).astype(jnp.bfloat16)


    tops = kept // 16 * 16

    recv1[0] = send1[chip]
    remote(recv1.at[others], recv1.at[others], 1, rs1, other).wait_recv()
    spectrum = mm(joined[...], recv1[...].reshape(chips * rank, block))
    power = jnp.sum(spectrum * spectrum, axis=1, keepdims=True)
    power = (power[:bins] + power[bins:]) / (2 * block)
    gain = lax.rsqrt(power + 1e-06)
    gath[chip] = (spectrum * jnp.concatenate([gain, gain], axis=0)).astype(jnp.bfloat16)
    for q in (*range(0, chips, 2), *range(1, chips, 2)):

        @pl.when(chip != q)
        def _():
            copy2(chip, q).start()

    picks = [pick.astype(jnp.float32) for pick in chosen]
    first_core = (core == 0).astype(jnp.float32)

    def weigh(rel, p):
        lines = recv1[slot(p), tops:].astype(jnp.float32)
        pair_lines = [lines[kept - tops + c : kept - tops + c + 1] for c in range(2)]
        own = pair_lines[rel] * first_core + pair_lines[1 - rel] * (1.0 - first_core)
        weight = jnp.zeros((1, 1), jnp.float32)
        for d in range(bands):
            weight = weight + own[:, d : d + 1] * picks[d]
        return jnp.broadcast_to(weight, (block, block)).astype(jnp.bfloat16)

    for q in range(chips):

        @pl.when(chip != q)
        def _():
            copy2(q, q).wait_recv()

        copy3(q).start()

    weights = [[weigh(rel, p) for p in range(chips)] for rel in range(2)]

    def turn(rel, first, last):
        tiles = [gath[rel * chips + u] * weights[rel][u] for u in range(first, last)]
        at = (rel * chips + first) * block
        turned[:, at : at + (last - first) * block] = jnp.transpose(
            jnp.concatenate(tiles, axis=0)
        )

    turn(0, 0, chips)
    for q in range(chips):
        copy3(q).wait_recv()
        turn(1, q, q + 1)
    rights = []
    for rel in range(2):
        for k in range(chips):
            later = jnp.minimum(k * 2 + (core + rel) % 2 + shift, n - 1)
            rights.append(gath[(later + core) % 2 * chips + later // 2])
    result = mm(turned[...], jnp.concatenate(rights, axis=0))
    out_ref[0] = result * (1.0 / (2 * bins))

    remote(pair, pair, 0, rs0.at[0], other).wait_send()
    some = gath.at[pl.ds(0, chips)]
    remote(some, some, 3, rs0.at[0], other).wait_send()
    remote(recv1.at[others], recv1.at[others], 1, rs0.at[0], other).wait_send()
    some = gath.at[others]
    remote(some, some, 2, rs0.at[0], other).wait_send()


def fused(raw, taps, tile_dist, tile_count, owner):
    n = lax.axis_size("chan")
    rows, channels = raw.shape
    bands = tile_dist.shape[1]
    block = channels // n
    steps = rows // 5
    chips = n // 2
    kept, rank = 40, 48
    lead = (128 - steps) // 2
    lefts, rights = window_factors(
        steps, lead, steps * n, steps * n // 16, (taps.shape[0] - 1) // 2, kept
    )
    spare = ((0, 0), (0, rank - kept), (0, 0))
    lefts, rights = np.pad(lefts, spare), np.pad(rights, spare)
    vmem, hbm = pl.BlockSpec(memory_space=pltpu.VMEM), pl.BlockSpec(memory_space=pltpu.HBM)
    dma = pltpu.SemaphoreType.DMA
    held = functools.partial(pltpu.with_memory_space_constraint, memory_space=pltpu.HBM)
    return pl.pallas_call(
        functools.partial(fused_kernel, n, bands, kept),
        out_shape=jax.ShapeDtypeStruct((1, block, block), jnp.float32),
        in_specs=[hbm] * 7,
        out_specs=vmem,
        scratch_shapes=[
            pltpu.VMEM(raw.shape, raw.dtype),
            pltpu.VMEM(taps.shape, taps.dtype),
            pltpu.SMEM(tile_dist.shape, jnp.int32),
            pltpu.SMEM(tile_count.shape, jnp.int32),
            pltpu.SMEM(owner.shape, jnp.int32),
            pltpu.VMEM(lefts.shape, jnp.float32),
            pltpu.VMEM(rights.shape[1:], jnp.float32),
            dma((2,)),
            dma((6,)),
            pltpu.VMEM((lefts.shape[2], chips * rank), jnp.bfloat16),
            pltpu.VMEM((n, rank, block), jnp.bfloat16),
            pltpu.VMEM((chips, rank, block), jnp.bfloat16),
            pltpu.VMEM((chips, rank, block), jnp.bfloat16),
            pltpu.VMEM((chips, rank, block), jnp.bfloat16),
            pltpu.VMEM((2 * chips, block, block), jnp.bfloat16),
            pltpu.VMEM((block, channels), jnp.bfloat16),
            pltpu.SemaphoreType.REGULAR,
            dma((4,)),
            dma((2,)),
            dma,
            dma((chips,)),
            dma((chips,)),
        ],
        compiler_params=pltpu.CompilerParams(
            collective_id=0, has_side_effects=True, vmem_limit_bytes=int(53.25 * 2**20)
        ),
    )(held(raw), held(taps), held(tile_dist), tile_count, held(owner), held(jnp.asarray(lefts)), held(jnp.asarray(rights)))


def shards(raw, taps, tile_dist, tile_count, owner):
    n = lax.axis_size("chan")
    rows, channels = raw.shape
    steps = rows // 5
    fits = (
        channels == 128 * n
        and n == 16
        and rows == 320
        and taps.shape[0] == 255
        and tile_dist.shape[1] == 4
    )
    path = fused if fits else streamed
    return path(raw, taps, tile_dist, tile_count, owner)


def solution(mesh):
    in_specs = (P("chan", "groups"), P(), P("chan", "groups"), P(("groups", "chan")), P("groups"))
    out_specs = P("chan", "groups", None)
    return jax.shard_map(shards, mesh=mesh, in_specs=in_specs, out_specs=out_specs, check_vma=False)
```

```python
import functools
import math

import jax
import jax.numpy as jnp
from jax import lax
from jax.experimental import pallas as pl
from jax.experimental.pallas import tpu as pltpu
from jax.sharding import PartitionSpec as P
import numpy as np

MESH = pl.DeviceIdType.MESH


def extended(x, sides, width):
    for axis, dim in sides:
        size, length = (lax.axis_size(axis), x.shape[dim])
        up = [(i, (i + 1) % size) for i in range(size - 1)]
        down = [(j, i) for i, j in up]
        last = lax.slice_in_dim(x, length - width, length, axis=dim)
        initial = lax.slice_in_dim(x, 0, width, axis=dim)
        before = lax.ppermute(last, axis, up)
        after = lax.ppermute(initial, axis, down)
        x = jnp.concatenate([before, x, after], axis=dim)
    return x


def passed_along(x, axis, by):
    size = lax.axis_size(axis)
    pairs = [(i, i + by) for i in range(size) if 0 <= i + by < size]
    return lax.ppermute(x, axis, pairs)


def band_matrix(taps, out_rows, in_cols):
    period = in_cols + 5
    padded = jnp.pad(taps, (0, period - taps.shape[0]))
    return jnp.tile(padded, out_rows)[: out_rows * in_cols].reshape(out_rows, in_cols)


def whiten(block):
    length, channels = block.shape
    bins = length // 16
    freqs = jnp.arange(1, bins + 1, dtype=jnp.int32)[:, None]
    times = jnp.arange(length, dtype=jnp.int32)[None, :]
    angle = (freqs * times % length).astype(jnp.float32) * (2.0 * math.pi / length)
    table = jnp.concatenate([jnp.cos(angle), -jnp.sin(angle)], axis=0)
    table_high = table.astype(jnp.bfloat16)
    table_low = (table - table_high.astype(jnp.float32)).astype(jnp.bfloat16)
    spectrum = jnp.dot(table_high, block, preferred_element_type=jnp.float32)
    spectrum = spectrum + jnp.dot(table_low, block, preferred_element_type=jnp.float32)
    squares = spectrum * spectrum
    power = jnp.sum(squares[:bins] + squares[bins:], axis=1) / (2 * channels)
    gain = lax.rsqrt(power + 1e-06)
    return (spectrum * jnp.concatenate([gain, gain])[:, None]).astype(jnp.bfloat16)


def cross_tile(mine, partner, scale):
    product = lax.dot_general(
        mine, partner, (((0,), (0,)), ((), ())), preferred_element_type=jnp.float32
    )
    return product * scale


def streamed(raw, taps, tile_dist, tile_count, owner):
    rows = raw.shape[0]
    width = taps.shape[0]
    half = (width - 1) // 2
    out_rows = rows // 5
    banded = band_matrix(taps, out_rows, rows + 2 * half)
    padded = extended(raw, (("chan", 0),), half)
    filtered = jnp.dot(banded, padded, preferred_element_type=jnp.float32)
    decimated = filtered.astype(jnp.bfloat16)
    regrouped = lax.all_to_all(decimated, "chan", split_axis=1, concat_axis=0, tiled=True)
    whitened = whiten(regrouped)
    channels = whitened.shape[1]
    scale = 1.0 / whitened.shape[0]
    bands = tile_dist.shape[1]
    slots = jnp.arange(bands, dtype=jnp.int32) < tile_count[0]
    stacks = []
    for distance in range(1, bands + 1):
        partner = passed_along(whitened, "chan", -distance)
        listed = jnp.sum(((tile_dist[0] == distance) & slots).astype(jnp.int32))
        tile = lax.cond(
            listed > 0,
            lambda first, second: cross_tile(first, second, scale),
            lambda first, second: jnp.zeros((channels, channels), jnp.float32),
            whitened,
            partner,
        )
        stacks.append(tile)
    stacked = jnp.stack(stacks)
    totals = lax.psum(stacked, "chan")
    selected = (owner == lax.axis_index("chan")).astype(jnp.float32)
    return jnp.einsum("b,bxy->xy", selected, totals, precision=lax.Precision.HIGHEST)[None]


def split(x):
    high = x.astype(jnp.bfloat16)
    low = (x - high.astype(jnp.float32)).astype(jnp.bfloat16)
    return high, low


def mm(a, b):
    return jnp.dot(a, b, preferred_element_type=jnp.float32)


def window_factors(steps, lead, length, bins, reach, rank):
    width = 2 * steps + 2 * lead
    chips = length // (2 * steps)
    freq = np.arange(1, bins + 1)[:, None]
    low, high = -(reach // 5), 2 * steps + (reach - 1) // 5 + 1
    time = np.arange(low, high)[None, :]

    def table(chip):
        angle = 2.0 * np.pi * ((freq * (time + 2 * steps * chip)) % length) / length
        return np.concatenate([np.cos(angle), -np.sin(angle)], axis=0)

    basis = np.linalg.svd(table(0), full_matrices=False)[2][:rank]
    lefts = np.stack([basis @ table(chip).T for chip in range(chips)])
    padded = np.zeros((rank, width))
    padded[:, lead + low : lead + high] = basis
    rights = np.stack([padded[:, c * steps : (c + 1) * steps + 2 * lead] for c in range(2)])
    return lefts.astype(np.float32), rights.astype(np.float32)


def fused_kernel(
    n, bands, kept,
    raw_hbm, taps_hbm, dist_hbm, count_hbm, owner_hbm, left_hbm, right_hbm, out_ref,
    raw_ref, taps_ref, dist_ref, count_ref, owner_ref, left_ref, right_ref, loads, smalls,
    joined, both, pair, send1, recv1, gath, turned, ready, sent, rs0, rs1, rs2, rs3,
):
    me = lax.axis_index("chan")
    chips = n // 2
    chip, core = me // 2, me % 2
    other = chip * 2 + 1 - core
    rows, channels = raw_ref.shape
    rank = right_ref.shape[0]
    block = channels // n
    steps = rows // 5
    length = steps * n
    bins = length // 16
    window = right_ref.shape[1]
    lead = (window - steps) // 2
    half = (taps_hbm.shape[0] - 1) // 2
    lanes = 1024
    start = lanes - 5 * lead - half
    cuts = 2
    cut = channels // cuts

    z, y = chip // 2, chip % 2

    def peer(k):
        far = [z, z + 1 - 2 * (z % 2), lax.rem(z + 2, 4), 3 - z][k // 2]
        return far * 2 + (1 - y if k % 2 else y)

    def slot(to):
        low = y + to % 2 - 2 * y * (to % 2)
        mid = z % 2 + to // 2 % 2 - 2 * (z % 2) * (to // 2 % 2)
        high = z // 2 + to // 4 - 2 * (z // 2) * (to // 4)
        return 4 * high + 2 * mid + low

    barrier = pltpu.get_barrier_semaphore()

    def greet(semaphore, to):
        pl.semaphore_signal(semaphore, inc=1, device_id={"chan": to}, device_id_type=MESH)

    @pl.when(core == 1)
    def _():
        greet(barrier, other)

    for q in range(chips):

        @pl.when(chip != q)
        def _():
            greet(barrier, q * 2 + 1)

    small = [
        pltpu.make_async_copy(source, held, smalls.at[at])
        for at, (source, held) in enumerate(
            [
                (taps_hbm, taps_ref),
                (right_hbm.at[core], right_ref),
                (dist_hbm, dist_ref),
                (count_hbm, count_ref),
                (owner_hbm, owner_ref),
                (left_hbm, left_ref),
            ]
        )
    ]
    for load in small[:4]:
        load.start()

    def load(c):
        cols = pl.ds(c * cut, cut)
        return pltpu.make_async_copy(raw_hbm.at[:, cols], raw_ref.at[:, cols], loads.at[c])

    for c in range(cuts):
        load(c).start()
    for load_one in small[4:]:
        load_one.start()

    for load_one in small[:2]:
        load_one.wait()
    tap = taps_ref[...].astype(jnp.float32).reshape(1, -1)
    line = jnp.concatenate(
        [
            jnp.zeros((1, start), jnp.float32),
            tap,
            jnp.zeros((1, lanes - start - tap.shape[1]), jnp.float32),
        ],
        axis=1,
    )
    first = pltpu.roll(jnp.broadcast_to(line, (8, lanes)), 0, 1, stride=5, stride_axis=0)
    banded = jnp.concatenate(
        [pltpu.roll(first, 40 * q, 1)[:, :384] for q in range(window // 8)], axis=0
    ).astype(jnp.bfloat16)[:, :rows]
    time = me * steps - lead + lax.broadcasted_iota(jnp.int32, (rank, window), 1)
    table = jnp.where((time >= 0) & (time < length), right_ref[...], 0.0)
    table_high, table_low = split(table)
    gmap = (mm(table_high, banded) + mm(table_low, banded)).astype(jnp.bfloat16)

    for load_one in small[2:4]:
        load_one.wait()
    line = lax.broadcasted_iota(jnp.int32, (rank, block), 0)
    lane = lax.broadcasted_iota(jnp.int32, (rank, block), 1)
    info = jnp.zeros((rank, block), jnp.float32)
    for d in range(bands):
        listed = jnp.int32(0)
        for s in range(bands):
            hit = (dist_ref[0, s] == d + 1) & (s < count_ref[0])
            listed = listed + hit.astype(jnp.int32)
        info = jnp.where((line == kept + core) & (lane == d), listed.astype(jnp.float32), info)

    def transform(c):
        load(c).wait()
        part = mm(gmap, raw_ref[:, c * cut : (c + 1) * cut])
        for j in range(cut // block):
            at = c * (cut // block) + j
            both[at % 2 * chips + at // 2] = (
                part[:, j * block : (j + 1) * block] + info
            ).astype(jnp.bfloat16)

    def remote(source, target, phase, sem, to):
        return pltpu.make_async_remote_copy(
            src_ref=source, dst_ref=target, send_sem=sent.at[phase], recv_sem=sem,
            device_id={"chan": to}, device_id_type=MESH,
        )

    def copy0(c):
        few = chips // cuts
        return remote(
            both.at[pl.ds((1 - core) * chips + c * few, few)], pair.at[pl.ds(c * few, few)],
            0, rs0.at[c], other,
        )

    def copy1(q):
        return remote(send1.at[q], recv1.at[slot(q)], 1, rs1, q * 2 + core)

    def copy2(source, to):
        return remote(gath.at[source], gath.at[source], 2, rs2.at[source], to * 2 + core)

    def copy3(q):
        return remote(gath.at[q], gath.at[chips + q], 3, rs3.at[q], other)

    others = pl.ds(1, chips - 1)

    @pl.when(core == 0)
    def _():
        pl.semaphore_wait(barrier, 1)
        greet(ready, other)

    for c in range(cuts):
        transform(c)
        if c == 0:

            @pl.when(core == 1)
            def _():
                pl.semaphore_wait(ready, 1)

        copy0(c).start()

    @pl.when(core == 1)
    def _():

        pl.semaphore_wait(barrier, 2 * (chips - 1))
        greet(ready, other)

    @pl.when(core == 0)
    def _():
        pl.semaphore_wait(ready, 1)

    for c in range(cuts):
        copy0(c).wait_recv()
    for q in range(chips - 1, -1, -1):
        own = both[core * chips + q].astype(jnp.float32)
        send1[q] = (own + pair[q].astype(jnp.float32)).astype(jnp.bfloat16)

        @pl.when(chip != q)
        def _():
            copy1(q).start()

    for load_one in small[4:]:
        load_one.wait()
    chosen = [(owner_ref[d] == me).astype(jnp.int32) for d in range(bands)]
    shift = sum((d + 1) * chosen[d] for d in range(bands))
    joined[...] = jnp.transpose(
        jnp.concatenate([left_ref[peer(k)] for k in range(chips)], axis=0)
    ).astype(jnp.bfloat16)


    tops = kept // 16 * 16

    recv1[0] = send1[chip]
    remote(recv1.at[others], recv1.at[others], 1, rs1, other).wait_recv()
    spectrum = mm(joined[...], recv1[...].reshape(chips * rank, block))
    power = jnp.sum(spectrum * spectrum, axis=1, keepdims=True)
    power = (power[:bins] + power[bins:]) / (2 * block)
    gain = lax.rsqrt(power + 1e-06)
    gath[chip] = (spectrum * jnp.concatenate([gain, gain], axis=0)).astype(jnp.bfloat16)
    @pl.when(chip != 0)
    def _():
        copy2(chip, 0).start()

    for k in range(1, chips):
        to = peer(k)

        @pl.when(to != 0)
        def _(to=to):
            copy2(chip, to).start()


    picks = [pick.astype(jnp.float32) for pick in chosen]
    first_core = (core == 0).astype(jnp.float32)

    def weigh(rel, p):
        lines = recv1[slot(p), tops:].astype(jnp.float32)
        pair_lines = [lines[kept - tops + c : kept - tops + c + 1] for c in range(2)]
        own = pair_lines[rel] * first_core + pair_lines[1 - rel] * (1.0 - first_core)
        weight = jnp.zeros((1, 1), jnp.float32)
        for d in range(bands):
            weight = weight + own[:, d : d + 1] * picks[d]
        return jnp.broadcast_to(weight, (block, block)).astype(jnp.bfloat16)

    for q in range(chips):

        @pl.when(chip != q)
        def _():
            copy2(q, q).wait_recv()

        copy3(q).start()

    weights = [[weigh(rel, p) for p in range(chips)] for rel in range(2)]

    def turn(rel, first, last):
        tiles = [gath[rel * chips + u] * weights[rel][u] for u in range(first, last)]
        at = (rel * chips + first) * block
        turned[:, at : at + (last - first) * block] = jnp.transpose(
            jnp.concatenate(tiles, axis=0)
        )

    turn(0, 0, chips)
    for q in range(chips):
        copy3(q).wait_recv()
        turn(1, q, q + 1)
    rights = []
    for rel in range(2):
        for k in range(chips):
            later = jnp.minimum(k * 2 + (core + rel) % 2 + shift, n - 1)
            rights.append(gath[(later + core) % 2 * chips + later // 2])
    result = mm(turned[...], jnp.concatenate(rights, axis=0))
    out_ref[0] = result * (1.0 / (2 * bins))

    remote(pair, pair, 0, rs0.at[0], other).wait_send()
    some = gath.at[pl.ds(0, chips)]
    remote(some, some, 3, rs0.at[0], other).wait_send()
    remote(recv1.at[others], recv1.at[others], 1, rs0.at[0], other).wait_send()
    some = gath.at[others]
    remote(some, some, 2, rs0.at[0], other).wait_send()


def fused(raw, taps, tile_dist, tile_count, owner):
    n = lax.axis_size("chan")
    rows, channels = raw.shape
    bands = tile_dist.shape[1]
    block = channels // n
    steps = rows // 5
    chips = n // 2
    kept, rank = 40, 48
    lead = (128 - steps) // 2
    lefts, rights = window_factors(
        steps, lead, steps * n, steps * n // 16, (taps.shape[0] - 1) // 2, kept
    )
    spare = ((0, 0), (0, rank - kept), (0, 0))
    lefts, rights = np.pad(lefts, spare), np.pad(rights, spare)
    vmem, hbm = pl.BlockSpec(memory_space=pltpu.VMEM), pl.BlockSpec(memory_space=pltpu.HBM)
    dma = pltpu.SemaphoreType.DMA
    held = functools.partial(pltpu.with_memory_space_constraint, memory_space=pltpu.HBM)
    return pl.pallas_call(
        functools.partial(fused_kernel, n, bands, kept),
        out_shape=jax.ShapeDtypeStruct((1, block, block), jnp.float32),
        in_specs=[hbm] * 7,
        out_specs=vmem,
        scratch_shapes=[
            pltpu.VMEM(raw.shape, raw.dtype),
            pltpu.VMEM(taps.shape, taps.dtype),
            pltpu.SMEM(tile_dist.shape, jnp.int32),
            pltpu.SMEM(tile_count.shape, jnp.int32),
            pltpu.SMEM(owner.shape, jnp.int32),
            pltpu.VMEM(lefts.shape, jnp.float32),
            pltpu.VMEM(rights.shape[1:], jnp.float32),
            dma((2,)),
            dma((6,)),
            pltpu.VMEM((lefts.shape[2], chips * rank), jnp.bfloat16),
            pltpu.VMEM((n, rank, block), jnp.bfloat16),
            pltpu.VMEM((chips, rank, block), jnp.bfloat16),
            pltpu.VMEM((chips, rank, block), jnp.bfloat16),
            pltpu.VMEM((chips, rank, block), jnp.bfloat16),
            pltpu.VMEM((2 * chips, block, block), jnp.bfloat16),
            pltpu.VMEM((block, channels), jnp.bfloat16),
            pltpu.SemaphoreType.REGULAR,
            dma((4,)),
            dma((2,)),
            dma,
            dma((chips,)),
            dma((chips,)),
        ],
        compiler_params=pltpu.CompilerParams(
            collective_id=0, has_side_effects=True, vmem_limit_bytes=int(53.25 * 2**20)
        ),
    )(held(raw), held(taps), held(tile_dist), tile_count, held(owner), held(jnp.asarray(lefts)), held(jnp.asarray(rights)))


def shards(raw, taps, tile_dist, tile_count, owner):
    n = lax.axis_size("chan")
    rows, channels = raw.shape
    steps = rows // 5
    fits = (
        channels == 128 * n
        and n == 16
        and rows == 320
        and taps.shape[0] == 255
        and tile_dist.shape[1] == 4
    )
    path = fused if fits else streamed
    return path(raw, taps, tile_dist, tile_count, owner)


def solution(mesh):
    in_specs = (P("chan", "groups"), P(), P("chan", "groups"), P(("groups", "chan")), P("groups"))
    out_specs = P("chan", "groups", None)
    return jax.shard_map(shards, mesh=mesh, in_specs=in_specs, out_specs=out_specs, check_vma=False)
```

```python
import functools
import math

import jax
import jax.numpy as jnp
from jax import lax
from jax.experimental import pallas as pl
from jax.experimental.pallas import tpu as pltpu
from jax.sharding import PartitionSpec as P
import numpy as np

MESH = pl.DeviceIdType.MESH


def extended(x, sides, width):
    for axis, dim in sides:
        size, length = (lax.axis_size(axis), x.shape[dim])
        up = [(i, (i + 1) % size) for i in range(size - 1)]
        down = [(j, i) for i, j in up]
        last = lax.slice_in_dim(x, length - width, length, axis=dim)
        initial = lax.slice_in_dim(x, 0, width, axis=dim)
        before = lax.ppermute(last, axis, up)
        after = lax.ppermute(initial, axis, down)
        x = jnp.concatenate([before, x, after], axis=dim)
    return x


def passed_along(x, axis, by):
    size = lax.axis_size(axis)
    pairs = [(i, i + by) for i in range(size) if 0 <= i + by < size]
    return lax.ppermute(x, axis, pairs)


def band_matrix(taps, out_rows, in_cols):
    period = in_cols + 5
    padded = jnp.pad(taps, (0, period - taps.shape[0]))
    return jnp.tile(padded, out_rows)[: out_rows * in_cols].reshape(out_rows, in_cols)


def whiten(block):
    length, channels = block.shape
    bins = length // 16
    freqs = jnp.arange(1, bins + 1, dtype=jnp.int32)[:, None]
    times = jnp.arange(length, dtype=jnp.int32)[None, :]
    angle = (freqs * times % length).astype(jnp.float32) * (2.0 * math.pi / length)
    table = jnp.concatenate([jnp.cos(angle), -jnp.sin(angle)], axis=0)
    table_high = table.astype(jnp.bfloat16)
    table_low = (table - table_high.astype(jnp.float32)).astype(jnp.bfloat16)
    spectrum = jnp.dot(table_high, block, preferred_element_type=jnp.float32)
    spectrum = spectrum + jnp.dot(table_low, block, preferred_element_type=jnp.float32)
    squares = spectrum * spectrum
    power = jnp.sum(squares[:bins] + squares[bins:], axis=1) / (2 * channels)
    gain = lax.rsqrt(power + 1e-06)
    return (spectrum * jnp.concatenate([gain, gain])[:, None]).astype(jnp.bfloat16)


def cross_tile(mine, partner, scale):
    product = lax.dot_general(
        mine, partner, (((0,), (0,)), ((), ())), preferred_element_type=jnp.float32
    )
    return product * scale


def streamed(raw, taps, tile_dist, tile_count, owner):
    rows = raw.shape[0]
    width = taps.shape[0]
    half = (width - 1) // 2
    out_rows = rows // 5
    banded = band_matrix(taps, out_rows, rows + 2 * half)
    padded = extended(raw, (("chan", 0),), half)
    filtered = jnp.dot(banded, padded, preferred_element_type=jnp.float32)
    decimated = filtered.astype(jnp.bfloat16)
    regrouped = lax.all_to_all(decimated, "chan", split_axis=1, concat_axis=0, tiled=True)
    whitened = whiten(regrouped)
    channels = whitened.shape[1]
    scale = 1.0 / whitened.shape[0]
    bands = tile_dist.shape[1]
    slots = jnp.arange(bands, dtype=jnp.int32) < tile_count[0]
    stacks = []
    for distance in range(1, bands + 1):
        partner = passed_along(whitened, "chan", -distance)
        listed = jnp.sum(((tile_dist[0] == distance) & slots).astype(jnp.int32))
        tile = lax.cond(
            listed > 0,
            lambda first, second: cross_tile(first, second, scale),
            lambda first, second: jnp.zeros((channels, channels), jnp.float32),
            whitened,
            partner,
        )
        stacks.append(tile)
    stacked = jnp.stack(stacks)
    totals = lax.psum(stacked, "chan")
    selected = (owner == lax.axis_index("chan")).astype(jnp.float32)
    return jnp.einsum("b,bxy->xy", selected, totals, precision=lax.Precision.HIGHEST)[None]


def split(x):
    high = x.astype(jnp.bfloat16)
    low = (x - high.astype(jnp.float32)).astype(jnp.bfloat16)
    return high, low


def mm(a, b):
    return jnp.dot(a, b, preferred_element_type=jnp.float32)


def window_factors(steps, lead, length, bins, reach, rank):
    width = 2 * steps + 2 * lead
    chips = length // (2 * steps)
    freq = np.arange(1, bins + 1)[:, None]
    low, high = -(reach // 5), 2 * steps + (reach - 1) // 5 + 1
    time = np.arange(low, high)[None, :]

    def table(chip):
        angle = 2.0 * np.pi * ((freq * (time + 2 * steps * chip)) % length) / length
        return np.concatenate([np.cos(angle), -np.sin(angle)], axis=0)

    basis = np.linalg.svd(table(0), full_matrices=False)[2][:rank]
    lefts = np.stack([basis @ table(chip).T for chip in range(chips)])
    padded = np.zeros((rank, width))
    padded[:, lead + low : lead + high] = basis
    rights = np.stack([padded[:, c * steps : (c + 1) * steps + 2 * lead] for c in range(2)])
    return lefts.astype(np.float32), rights.astype(np.float32)


def fused_kernel(
    n, bands, kept,
    raw_hbm, taps_hbm, dist_hbm, count_hbm, owner_hbm, left_hbm, right_hbm, out_ref,
    raw_ref, taps_ref, dist_ref, count_ref, owner_ref, left_ref, right_ref, loads, smalls,
    joined, both, pair, send1, recv1, gath, ready, sent, rs0, rs1, rs2, rs3,
):
    me = lax.axis_index("chan")
    chips = n // 2
    chip, core = me // 2, me % 2
    other = chip * 2 + 1 - core
    rows, channels = raw_ref.shape
    rank = right_ref.shape[0]
    block = channels // n
    steps = rows // 5
    length = steps * n
    bins = length // 16
    window = right_ref.shape[1]
    lead = (window - steps) // 2
    half = (taps_hbm.shape[0] - 1) // 2
    lanes = 1024
    start = lanes - 5 * lead - half
    cuts = 2
    cut = channels // cuts

    z, y = chip // 2, chip % 2

    def peer(k):
        far = [z, z + 1 - 2 * (z % 2), lax.rem(z + 2, 4), 3 - z][k // 2]
        return far * 2 + (1 - y if k % 2 else y)

    def slot(to):
        low = y + to % 2 - 2 * y * (to % 2)
        mid = z % 2 + to // 2 % 2 - 2 * (z % 2) * (to // 2 % 2)
        high = z // 2 + to // 4 - 2 * (z // 2) * (to // 4)
        return 4 * high + 2 * mid + low

    barrier = pltpu.get_barrier_semaphore()

    def greet(semaphore, to):
        pl.semaphore_signal(semaphore, inc=1, device_id={"chan": to}, device_id_type=MESH)

    @pl.when(core == 1)
    def _():
        greet(barrier, other)

    for q in range(chips):

        @pl.when(chip != q)
        def _():
            greet(barrier, q * 2 + 1)

    small = [
        pltpu.make_async_copy(source, held, smalls.at[at])
        for at, (source, held) in enumerate(
            [
                (taps_hbm, taps_ref),
                (right_hbm.at[core], right_ref),
                (dist_hbm, dist_ref),
                (count_hbm, count_ref),
                (owner_hbm, owner_ref),
                (left_hbm, left_ref),
            ]
        )
    ]
    for load in small[:4]:
        load.start()

    def load(c):
        cols = pl.ds(c * cut, cut)
        return pltpu.make_async_copy(raw_hbm.at[:, cols], raw_ref.at[:, cols], loads.at[c])

    for c in range(cuts):
        load(c).start()
    for load_one in small[4:]:
        load_one.start()

    for load_one in small[:2]:
        load_one.wait()
    tap = taps_ref[...].astype(jnp.float32).reshape(1, -1)
    line = jnp.concatenate(
        [
            jnp.zeros((1, start), jnp.float32),
            tap,
            jnp.zeros((1, lanes - start - tap.shape[1]), jnp.float32),
        ],
        axis=1,
    )
    first = pltpu.roll(jnp.broadcast_to(line, (8, lanes)), 0, 1, stride=5, stride_axis=0)
    banded = jnp.concatenate(
        [pltpu.roll(first, 40 * q, 1)[:, :384] for q in range(window // 8)], axis=0
    ).astype(jnp.bfloat16)[:, :rows]
    time = me * steps - lead + lax.broadcasted_iota(jnp.int32, (rank, window), 1)
    table = jnp.where((time >= 0) & (time < length), right_ref[...], 0.0)
    table_high, table_low = split(table)
    gmap = (mm(table_high, banded) + mm(table_low, banded)).astype(jnp.bfloat16)

    for load_one in small[2:4]:
        load_one.wait()
    line = lax.broadcasted_iota(jnp.int32, (rank, block), 0)
    lane = lax.broadcasted_iota(jnp.int32, (rank, block), 1)
    info = jnp.zeros((rank, block), jnp.float32)
    for d in range(bands):
        listed = jnp.int32(0)
        for s in range(bands):
            hit = (dist_ref[0, s] == d + 1) & (s < count_ref[0])
            listed = listed + hit.astype(jnp.int32)
        info = jnp.where((line == kept + core) & (lane == d), listed.astype(jnp.float32), info)

    def transform(c):
        load(c).wait()
        part = mm(gmap, raw_ref[:, c * cut : (c + 1) * cut])
        for j in range(cut // block):
            at = c * (cut // block) + j
            both[at % 2 * chips + at // 2] = (
                part[:, j * block : (j + 1) * block] + info
            ).astype(jnp.bfloat16)

    def remote(source, target, phase, sem, to):
        return pltpu.make_async_remote_copy(
            src_ref=source, dst_ref=target, send_sem=sent.at[phase], recv_sem=sem,
            device_id={"chan": to}, device_id_type=MESH,
        )

    def copy0(c):
        few = chips // cuts
        return remote(
            both.at[pl.ds((1 - core) * chips + c * few, few)], pair.at[pl.ds(c * few, few)],
            0, rs0.at[c], other,
        )

    def copy1(q):
        return remote(send1.at[q], recv1.at[slot(q)], 1, rs1, q * 2 + core)

    def copy2(source, to):
        return remote(gath.at[source], gath.at[source], 2, rs2.at[source], to * 2 + core)

    def copy3(q):
        return remote(gath.at[q], gath.at[chips + q], 3, rs3.at[q], other)

    others = pl.ds(1, chips - 1)

    @pl.when(core == 0)
    def _():
        pl.semaphore_wait(barrier, 1)
        greet(ready, other)

    for c in range(cuts):
        transform(c)
        if c == 0:

            @pl.when(core == 1)
            def _():
                pl.semaphore_wait(ready, 1)

        copy0(c).start()

    @pl.when(core == 1)
    def _():

        pl.semaphore_wait(barrier, 2 * (chips - 1))
        greet(ready, other)

    @pl.when(core == 0)
    def _():
        pl.semaphore_wait(ready, 1)

    for c in range(cuts):
        copy0(c).wait_recv()
    for q in range(chips - 1, -1, -1):
        own = both[core * chips + q].astype(jnp.float32)
        send1[q] = (own + pair[q].astype(jnp.float32)).astype(jnp.bfloat16)

        @pl.when(chip != q)
        def _():
            copy1(q).start()

    for load_one in small[4:]:
        load_one.wait()
    chosen = [(owner_ref[d] == me).astype(jnp.int32) for d in range(bands)]
    shift = sum((d + 1) * chosen[d] for d in range(bands))
    joined[...] = jnp.transpose(
        jnp.concatenate([left_ref[peer(k)] for k in range(chips)], axis=0)
    ).astype(jnp.bfloat16)


    tops = kept // 16 * 16

    recv1[0] = send1[chip]
    remote(recv1.at[others], recv1.at[others], 1, rs1, other).wait_recv()
    spectrum = mm(joined[...], recv1[...].reshape(chips * rank, block))
    power = jnp.sum(spectrum * spectrum, axis=1, keepdims=True)
    power = (power[:bins] + power[bins:]) / (2 * block)
    gain = lax.rsqrt(power + 1e-06)
    gath[chip] = (spectrum * jnp.concatenate([gain, gain], axis=0)).astype(jnp.bfloat16)
    @pl.when(chip != 0)
    def _():
        copy2(chip, 0).start()

    for k in range(1, chips):
        to = peer(k)

        @pl.when(to != 0)
        def _(to=to):
            copy2(chip, to).start()


    picks = [pick.astype(jnp.float32) for pick in chosen]
    first_core = (core == 0).astype(jnp.float32)

    def weigh(rel, p):
        lines = recv1[slot(p), tops:].astype(jnp.float32)
        pair_lines = [lines[kept - tops + c : kept - tops + c + 1] for c in range(2)]
        own = pair_lines[rel] * first_core + pair_lines[1 - rel] * (1.0 - first_core)
        weight = jnp.zeros((1, 1), jnp.float32)
        for d in range(bands):
            weight = weight + own[:, d : d + 1] * picks[d]
        return jnp.broadcast_to(weight, (block, block)).astype(jnp.bfloat16)

    for q in range(chips):

        @pl.when(chip != q)
        def _():
            copy2(q, q).wait_recv()

        copy3(q).start()

    weights = [[weigh(rel, p) for p in range(chips)] for rel in range(2)]

    for q in range(chips):
        copy3(q).wait_recv()
    lefts, rights = [], []
    for rel in range(2):
        for k in range(chips):
            lefts.append(gath[rel * chips + k] * weights[rel][k])
            later = jnp.minimum(k * 2 + (core + rel) % 2 + shift, n - 1)
            rights.append(gath[(later + core) % 2 * chips + later // 2])
    result = lax.dot_general(
        jnp.concatenate(lefts, axis=0), jnp.concatenate(rights, axis=0),
        (((0,), (0,)), ((), ())), preferred_element_type=jnp.float32,
    )
    out_ref[0] = result * (1.0 / (2 * bins))

    remote(pair, pair, 0, rs0.at[0], other).wait_send()
    some = gath.at[pl.ds(0, chips)]
    remote(some, some, 3, rs0.at[0], other).wait_send()
    remote(recv1.at[others], recv1.at[others], 1, rs0.at[0], other).wait_send()
    some = gath.at[others]
    remote(some, some, 2, rs0.at[0], other).wait_send()


def fused(raw, taps, tile_dist, tile_count, owner):
    n = lax.axis_size("chan")
    rows, channels = raw.shape
    bands = tile_dist.shape[1]
    block = channels // n
    steps = rows // 5
    chips = n // 2
    kept, rank = 40, 48
    lead = (128 - steps) // 2
    lefts, rights = window_factors(
        steps, lead, steps * n, steps * n // 16, (taps.shape[0] - 1) // 2, kept
    )
    spare = ((0, 0), (0, rank - kept), (0, 0))
    lefts, rights = np.pad(lefts, spare), np.pad(rights, spare)
    vmem, hbm = pl.BlockSpec(memory_space=pltpu.VMEM), pl.BlockSpec(memory_space=pltpu.HBM)
    dma = pltpu.SemaphoreType.DMA
    held = functools.partial(pltpu.with_memory_space_constraint, memory_space=pltpu.HBM)
    return pl.pallas_call(
        functools.partial(fused_kernel, n, bands, kept),
        out_shape=jax.ShapeDtypeStruct((1, block, block), jnp.float32),
        in_specs=[hbm] * 7,
        out_specs=vmem,
        scratch_shapes=[
            pltpu.VMEM(raw.shape, raw.dtype),
            pltpu.VMEM(taps.shape, taps.dtype),
            pltpu.SMEM(tile_dist.shape, jnp.int32),
            pltpu.SMEM(tile_count.shape, jnp.int32),
            pltpu.SMEM(owner.shape, jnp.int32),
            pltpu.VMEM(lefts.shape, jnp.float32),
            pltpu.VMEM(rights.shape[1:], jnp.float32),
            dma((2,)),
            dma((6,)),
            pltpu.VMEM((lefts.shape[2], chips * rank), jnp.bfloat16),
            pltpu.VMEM((n, rank, block), jnp.bfloat16),
            pltpu.VMEM((chips, rank, block), jnp.bfloat16),
            pltpu.VMEM((chips, rank, block), jnp.bfloat16),
            pltpu.VMEM((chips, rank, block), jnp.bfloat16),
            pltpu.VMEM((2 * chips, block, block), jnp.bfloat16),
            pltpu.SemaphoreType.REGULAR,
            dma((4,)),
            dma((2,)),
            dma,
            dma((chips,)),
            dma((chips,)),
        ],
        compiler_params=pltpu.CompilerParams(
            collective_id=0, has_side_effects=True, vmem_limit_bytes=int(53.25 * 2**20)
        ),
    )(held(raw), held(taps), held(tile_dist), tile_count, held(owner), held(jnp.asarray(lefts)), held(jnp.asarray(rights)))


def shards(raw, taps, tile_dist, tile_count, owner):
    n = lax.axis_size("chan")
    rows, channels = raw.shape
    steps = rows // 5
    fits = (
        channels == 128 * n
        and n == 16
        and rows == 320
        and taps.shape[0] == 255
        and tile_dist.shape[1] == 4
    )
    path = fused if fits else streamed
    return path(raw, taps, tile_dist, tile_count, owner)


def solution(mesh):
    in_specs = (P("chan", "groups"), P(), P("chan", "groups"), P(("groups", "chan")), P("groups"))
    out_specs = P("chan", "groups", None)
    return jax.shard_map(shards, mesh=mesh, in_specs=in_specs, out_specs=out_specs, check_vma=False)
```

```python
import functools
import math

import jax
import jax.numpy as jnp
from jax import lax
from jax.experimental import pallas as pl
from jax.experimental.pallas import tpu as pltpu
from jax.sharding import PartitionSpec as P
import numpy as np

MESH = pl.DeviceIdType.MESH


def extended(x, sides, width):
    for axis, dim in sides:
        size, length = (lax.axis_size(axis), x.shape[dim])
        up = [(i, (i + 1) % size) for i in range(size - 1)]
        down = [(j, i) for i, j in up]
        last = lax.slice_in_dim(x, length - width, length, axis=dim)
        initial = lax.slice_in_dim(x, 0, width, axis=dim)
        before = lax.ppermute(last, axis, up)
        after = lax.ppermute(initial, axis, down)
        x = jnp.concatenate([before, x, after], axis=dim)
    return x


def passed_along(x, axis, by):
    size = lax.axis_size(axis)
    pairs = [(i, i + by) for i in range(size) if 0 <= i + by < size]
    return lax.ppermute(x, axis, pairs)


def band_matrix(taps, out_rows, in_cols):
    period = in_cols + 5
    padded = jnp.pad(taps, (0, period - taps.shape[0]))
    return jnp.tile(padded, out_rows)[: out_rows * in_cols].reshape(out_rows, in_cols)


def whiten(block):
    length, channels = block.shape
    bins = length // 16
    freqs = jnp.arange(1, bins + 1, dtype=jnp.int32)[:, None]
    times = jnp.arange(length, dtype=jnp.int32)[None, :]
    angle = (freqs * times % length).astype(jnp.float32) * (2.0 * math.pi / length)
    table = jnp.concatenate([jnp.cos(angle), -jnp.sin(angle)], axis=0)
    table_high = table.astype(jnp.bfloat16)
    table_low = (table - table_high.astype(jnp.float32)).astype(jnp.bfloat16)
    spectrum = jnp.dot(table_high, block, preferred_element_type=jnp.float32)
    spectrum = spectrum + jnp.dot(table_low, block, preferred_element_type=jnp.float32)
    squares = spectrum * spectrum
    power = jnp.sum(squares[:bins] + squares[bins:], axis=1) / (2 * channels)
    gain = lax.rsqrt(power + 1e-06)
    return (spectrum * jnp.concatenate([gain, gain])[:, None]).astype(jnp.bfloat16)


def cross_tile(mine, partner, scale):
    product = lax.dot_general(
        mine, partner, (((0,), (0,)), ((), ())), preferred_element_type=jnp.float32
    )
    return product * scale


def streamed(raw, taps, tile_dist, tile_count, owner):
    rows = raw.shape[0]
    width = taps.shape[0]
    half = (width - 1) // 2
    out_rows = rows // 5
    banded = band_matrix(taps, out_rows, rows + 2 * half)
    padded = extended(raw, (("chan", 0),), half)
    filtered = jnp.dot(banded, padded, preferred_element_type=jnp.float32)
    decimated = filtered.astype(jnp.bfloat16)
    regrouped = lax.all_to_all(decimated, "chan", split_axis=1, concat_axis=0, tiled=True)
    whitened = whiten(regrouped)
    channels = whitened.shape[1]
    scale = 1.0 / whitened.shape[0]
    bands = tile_dist.shape[1]
    slots = jnp.arange(bands, dtype=jnp.int32) < tile_count[0]
    stacks = []
    for distance in range(1, bands + 1):
        partner = passed_along(whitened, "chan", -distance)
        listed = jnp.sum(((tile_dist[0] == distance) & slots).astype(jnp.int32))
        tile = lax.cond(
            listed > 0,
            lambda first, second: cross_tile(first, second, scale),
            lambda first, second: jnp.zeros((channels, channels), jnp.float32),
            whitened,
            partner,
        )
        stacks.append(tile)
    stacked = jnp.stack(stacks)
    totals = lax.psum(stacked, "chan")
    selected = (owner == lax.axis_index("chan")).astype(jnp.float32)
    return jnp.einsum("b,bxy->xy", selected, totals, precision=lax.Precision.HIGHEST)[None]


def split(x):
    high = x.astype(jnp.bfloat16)
    low = (x - high.astype(jnp.float32)).astype(jnp.bfloat16)
    return high, low


def mm(a, b):
    return jnp.dot(a, b, preferred_element_type=jnp.float32)


def window_factors(steps, lead, length, bins, reach, rank):
    width = 2 * steps + 2 * lead
    chips = length // (2 * steps)
    freq = np.arange(1, bins + 1)[:, None]
    low, high = -(reach // 5), 2 * steps + (reach - 1) // 5 + 1
    time = np.arange(low, high)[None, :]

    def table(chip):
        angle = 2.0 * np.pi * ((freq * (time + 2 * steps * chip)) % length) / length
        return np.concatenate([np.cos(angle), -np.sin(angle)], axis=0)

    basis = np.linalg.svd(table(0), full_matrices=False)[2][:rank]
    lefts = np.stack([basis @ table(chip).T for chip in range(chips)])
    padded = np.zeros((rank, width))
    padded[:, lead + low : lead + high] = basis
    rights = np.stack([padded[:, c * steps : (c + 1) * steps + 2 * lead] for c in range(2)])
    return lefts.astype(np.float32), rights.astype(np.float32)


def fused_kernel(
    n, bands, kept,
    raw_hbm, taps_hbm, dist_hbm, count_hbm, owner_hbm, left_hbm, right_hbm, out_ref,
    raw_ref, taps_ref, dist_ref, count_ref, owner_ref, left_ref, right_ref, loads, smalls,
    joined, both, pair, send1, recv1, gath, ready, sent, rs0, rs1, rs2, rs3,
):
    me = lax.axis_index("chan")
    chips = n // 2
    chip, core = me // 2, me % 2
    other = chip * 2 + 1 - core
    rows, channels = raw_ref.shape
    rank = right_ref.shape[0]
    block = channels // n
    steps = rows // 5
    length = steps * n
    bins = length // 16
    window = right_ref.shape[1]
    lead = (window - steps) // 2
    half = (taps_hbm.shape[0] - 1) // 2
    lanes = 1024
    start = lanes - 5 * lead - half
    cuts = 2
    cut = channels // cuts

    z, y = chip // 2, chip % 2

    def peer(k):
        far = [z, z + 1 - 2 * (z % 2), lax.rem(z + 2, 4), 3 - z][k // 2]
        return far * 2 + (1 - y if k % 2 else y)

    def slot(to):
        low = y + to % 2 - 2 * y * (to % 2)
        mid = z % 2 + to // 2 % 2 - 2 * (z % 2) * (to // 2 % 2)
        high = z // 2 + to // 4 - 2 * (z // 2) * (to // 4)
        return 4 * high + 2 * mid + low

    barrier = pltpu.get_barrier_semaphore()

    def greet(semaphore, to):
        pl.semaphore_signal(semaphore, inc=1, device_id={"chan": to}, device_id_type=MESH)

    @pl.when(core == 1)
    def _():
        greet(barrier, other)

    for q in range(chips):

        @pl.when(chip != q)
        def _():
            greet(barrier, q * 2 + 1)

    small = [
        pltpu.make_async_copy(source, held, smalls.at[at])
        for at, (source, held) in enumerate(
            [
                (taps_hbm, taps_ref),
                (right_hbm.at[core], right_ref),
                (dist_hbm, dist_ref),
                (count_hbm, count_ref),
                (owner_hbm, owner_ref),
                (left_hbm, left_ref),
            ]
        )
    ]
    for load in small[:4]:
        load.start()

    def load(c):
        cols = pl.ds(c * cut, cut)
        return pltpu.make_async_copy(raw_hbm.at[:, cols], raw_ref.at[:, cols], loads.at[c])

    for c in range(cuts):
        load(c).start()
    for load_one in small[4:]:
        load_one.start()

    for load_one in small[:2]:
        load_one.wait()
    tap = taps_ref[...].astype(jnp.float32).reshape(1, -1)
    line = jnp.concatenate(
        [
            jnp.zeros((1, start), jnp.float32),
            tap,
            jnp.zeros((1, lanes - start - tap.shape[1]), jnp.float32),
        ],
        axis=1,
    )
    first = pltpu.roll(jnp.broadcast_to(line, (8, lanes)), 0, 1, stride=5, stride_axis=0)
    banded = jnp.concatenate(
        [pltpu.roll(first, 40 * q, 1)[:, :384] for q in range(window // 8)], axis=0
    ).astype(jnp.bfloat16)[:, :rows]
    time = me * steps - lead + lax.broadcasted_iota(jnp.int32, (rank, window), 1)
    table = jnp.where((time >= 0) & (time < length), right_ref[...], 0.0)
    table_high, table_low = split(table)
    gmap = (mm(table_high, banded) + mm(table_low, banded)).astype(jnp.bfloat16)

    for load_one in small[2:4]:
        load_one.wait()
    line = lax.broadcasted_iota(jnp.int32, (rank, block), 0)
    lane = lax.broadcasted_iota(jnp.int32, (rank, block), 1)
    info = jnp.zeros((rank, block), jnp.float32)
    for d in range(bands):
        listed = jnp.int32(0)
        for s in range(bands):
            hit = (dist_ref[0, s] == d + 1) & (s < count_ref[0])
            listed = listed + hit.astype(jnp.int32)
        info = jnp.where((line == kept + core) & (lane == d), listed.astype(jnp.float32), info)

    def transform(c):
        load(c).wait()
        part = mm(gmap, raw_ref[:, c * cut : (c + 1) * cut])
        for j in range(cut // block):
            at = c * (cut // block) + j
            both[at % 2 * chips + at // 2] = (
                part[:, j * block : (j + 1) * block] + info
            ).astype(jnp.bfloat16)

    def remote(source, target, phase, sem, to):
        return pltpu.make_async_remote_copy(
            src_ref=source, dst_ref=target, send_sem=sent.at[phase], recv_sem=sem,
            device_id={"chan": to}, device_id_type=MESH,
        )

    def copy0(c):
        few = chips // cuts
        return remote(
            both.at[pl.ds((1 - core) * chips + c * few, few)], pair.at[pl.ds(c * few, few)],
            0, rs0.at[c], other,
        )

    def copy1(q):
        return remote(send1.at[q], recv1.at[slot(q)], 1, rs1, q * 2 + core)

    def copy2(source, to):
        return remote(gath.at[source], gath.at[source], 2, rs2.at[source], to * 2 + core)

    def copy3(q):
        here, there = pl.ds(2 * q, 2), pl.ds(chips + 2 * q, 2)
        return remote(gath.at[here], gath.at[there], 3, rs3.at[q], other)

    others = pl.ds(1, chips - 1)

    @pl.when(core == 0)
    def _():
        pl.semaphore_wait(barrier, 1)
        greet(ready, other)

    for c in range(cuts):
        transform(c)
        if c == 0:

            @pl.when(core == 1)
            def _():
                pl.semaphore_wait(ready, 1)

        copy0(c).start()

    @pl.when(core == 1)
    def _():

        pl.semaphore_wait(barrier, 2 * (chips - 1))
        greet(ready, other)

    @pl.when(core == 0)
    def _():
        pl.semaphore_wait(ready, 1)

    for c in range(cuts):
        copy0(c).wait_recv()
    for q in range(chips - 1, -1, -1):
        own = both[core * chips + q].astype(jnp.float32)
        send1[q] = (own + pair[q].astype(jnp.float32)).astype(jnp.bfloat16)

        @pl.when(chip != q)
        def _():
            copy1(q).start()

    for load_one in small[4:]:
        load_one.wait()
    chosen = [(owner_ref[d] == me).astype(jnp.int32) for d in range(bands)]
    shift = sum((d + 1) * chosen[d] for d in range(bands))
    joined[...] = jnp.transpose(
        jnp.concatenate([left_ref[peer(k)] for k in range(chips)], axis=0)
    ).astype(jnp.bfloat16)


    tops = kept // 16 * 16

    recv1[0] = send1[chip]
    remote(recv1.at[others], recv1.at[others], 1, rs1, other).wait_recv()
    spectrum = mm(joined[...], recv1[...].reshape(chips * rank, block))
    power = jnp.sum(spectrum * spectrum, axis=1, keepdims=True)
    power = (power[:bins] + power[bins:]) / (2 * block)
    gain = lax.rsqrt(power + 1e-06)
    gath[chip] = (spectrum * jnp.concatenate([gain, gain], axis=0)).astype(jnp.bfloat16)
    @pl.when(chip != 0)
    def _():
        copy2(chip, 0).start()

    for k in range(1, chips):
        to = peer(k)

        @pl.when(to != 0)
        def _(to=to):
            copy2(chip, to).start()


    picks = [pick.astype(jnp.float32) for pick in chosen]
    first_core = (core == 0).astype(jnp.float32)

    def weigh(rel, p):
        lines = recv1[slot(p), tops:].astype(jnp.float32)
        pair_lines = [lines[kept - tops + c : kept - tops + c + 1] for c in range(2)]
        own = pair_lines[rel] * first_core + pair_lines[1 - rel] * (1.0 - first_core)
        weight = jnp.zeros((1, 1), jnp.float32)
        for d in range(bands):
            weight = weight + own[:, d : d + 1] * picks[d]
        return jnp.broadcast_to(weight, (block, block)).astype(jnp.bfloat16)

    for q in range(chips):

        @pl.when(chip != q)
        def _():
            copy2(q, q).wait_recv()

        if q % 2:
            copy3(q // 2).start()

    weights = [[weigh(rel, p) for p in range(chips)] for rel in range(2)]

    for q in range(chips // 2):
        copy3(q).wait_recv()
    lefts, rights = [], []
    for rel in range(2):
        for k in range(chips):
            lefts.append(gath[rel * chips + k] * weights[rel][k])
            later = jnp.minimum(k * 2 + (core + rel) % 2 + shift, n - 1)
            rights.append(gath[(later + core) % 2 * chips + later // 2])
    result = lax.dot_general(
        jnp.concatenate(lefts, axis=0), jnp.concatenate(rights, axis=0),
        (((0,), (0,)), ((), ())), preferred_element_type=jnp.float32,
    )
    out_ref[0] = result * (1.0 / (2 * bins))

    remote(pair, pair, 0, rs0.at[0], other).wait_send()
    some = gath.at[pl.ds(0, chips)]
    remote(some, some, 3, rs0.at[0], other).wait_send()
    remote(recv1.at[others], recv1.at[others], 1, rs0.at[0], other).wait_send()
    some = gath.at[others]
    remote(some, some, 2, rs0.at[0], other).wait_send()


def fused(raw, taps, tile_dist, tile_count, owner):
    n = lax.axis_size("chan")
    rows, channels = raw.shape
    bands = tile_dist.shape[1]
    block = channels // n
    steps = rows // 5
    chips = n // 2
    kept, rank = 40, 48
    lead = (128 - steps) // 2
    lefts, rights = window_factors(
        steps, lead, steps * n, steps * n // 16, (taps.shape[0] - 1) // 2, kept
    )
    spare = ((0, 0), (0, rank - kept), (0, 0))
    lefts, rights = np.pad(lefts, spare), np.pad(rights, spare)
    vmem, hbm = pl.BlockSpec(memory_space=pltpu.VMEM), pl.BlockSpec(memory_space=pltpu.HBM)
    dma = pltpu.SemaphoreType.DMA
    held = functools.partial(pltpu.with_memory_space_constraint, memory_space=pltpu.HBM)
    return pl.pallas_call(
        functools.partial(fused_kernel, n, bands, kept),
        out_shape=jax.ShapeDtypeStruct((1, block, block), jnp.float32),
        in_specs=[hbm] * 7,
        out_specs=vmem,
        scratch_shapes=[
            pltpu.VMEM(raw.shape, raw.dtype),
            pltpu.VMEM(taps.shape, taps.dtype),
            pltpu.SMEM(tile_dist.shape, jnp.int32),
            pltpu.SMEM(tile_count.shape, jnp.int32),
            pltpu.SMEM(owner.shape, jnp.int32),
            pltpu.VMEM(lefts.shape, jnp.float32),
            pltpu.VMEM(rights.shape[1:], jnp.float32),
            dma((2,)),
            dma((6,)),
            pltpu.VMEM((lefts.shape[2], chips * rank), jnp.bfloat16),
            pltpu.VMEM((n, rank, block), jnp.bfloat16),
            pltpu.VMEM((chips, rank, block), jnp.bfloat16),
            pltpu.VMEM((chips, rank, block), jnp.bfloat16),
            pltpu.VMEM((chips, rank, block), jnp.bfloat16),
            pltpu.VMEM((2 * chips, block, block), jnp.bfloat16),
            pltpu.SemaphoreType.REGULAR,
            dma((4,)),
            dma((2,)),
            dma,
            dma((chips,)),
            dma((chips // 2,)),
        ],
        compiler_params=pltpu.CompilerParams(
            collective_id=0, has_side_effects=True, vmem_limit_bytes=int(53.25 * 2**20)
        ),
    )(held(raw), held(taps), held(tile_dist), tile_count, held(owner), held(jnp.asarray(lefts)), held(jnp.asarray(rights)))


def shards(raw, taps, tile_dist, tile_count, owner):
    n = lax.axis_size("chan")
    rows, channels = raw.shape
    steps = rows // 5
    fits = (
        channels == 128 * n
        and n == 16
        and rows == 320
        and taps.shape[0] == 255
        and tile_dist.shape[1] == 4
    )
    path = fused if fits else streamed
    return path(raw, taps, tile_dist, tile_count, owner)


def solution(mesh):
    in_specs = (P("chan", "groups"), P(), P("chan", "groups"), P(("groups", "chan")), P("groups"))
    out_specs = P("chan", "groups", None)
    return jax.shard_map(shards, mesh=mesh, in_specs=in_specs, out_specs=out_specs, check_vma=False)
```
